256 devices in a mesh: prow: 16 (over x, y), pcol: 16 (over z, core).
Axes of the slice: x: 4, y: 4, z: 8, core: 2. Of those that a mesh axis runs over, the one named last changes fastest.
Arguments:
- diag_inverse: float32 [2, 1024, 1024], P(None, 'pcol', 'prow'), as said below
- coupling: float32 [1024, 1024], P('prow', 'pcol'), may hold values from -0.1875 to 0.1875
- rhs_top: float32 [2, 1024, 1024], P(None, 'prow'), may hold values from -6 to 6
- panel: float32 [65536, 2048], P('prow', 'pcol'), may hold values from -0.1875 to 0.1875
- rhs_rest: float32 [65536, 1024], P(('prow', 'pcol')), may hold values from -6 to 6
Outputs:
- adjoint_top: float32 [2, 1024, 1024], P(None, 'pcol')
- rhs_updated: float32 [65536, 1024], P(('prow', 'pcol'))
The draws below stay inside these ranges and needn't reach their ends.
Inputs may be any that keep to these rules, and one draw needn't show every extreme that they name: Each of the two blocks of diag_inverse is lower triangular, with zeros above the diagonal.
All inputs are finite; a program needn't handle non-finite values.
Results may differ from the reference program's by a relative error of at most 0.000065.
Values sent between devices are 32-bit elements; how exact they have to be, the bound alone decides.
A program may use at most 64 MiB of HBM per device.

```python
import jax
import jax.numpy as jnp
from jax import lax

BLOCK = 1024
ADJOINTS = 1024
COL_TILE = 64
TRAIL_ROWS = 65536
N_PCOL = 16


def draw_diag_inverse(key, part):
    key = jax.random.fold_in(key, 11)
    key_off, key_mag, key_sign = jax.random.split(key, 3)
    spread = jax.random.normal(key_off, (2, BLOCK, BLOCK), jnp.float32)
    magnitude = jax.random.uniform(key_mag, (2, BLOCK), jnp.float32, 0.7, 1.5)
    signs = (jax.random.randint(key_sign, (2, BLOCK), 0, 2) * 2 - 1).astype(jnp.float32)
    row_index = lax.broadcasted_iota(jnp.int32, (BLOCK, BLOCK), 0)
    col_index = lax.broadcasted_iota(jnp.int32, (BLOCK, BLOCK), 1)
    below = (row_index > col_index)[None]
    on_diag = (row_index == col_index)[None]
    scaled = spread * (0.8 / BLOCK ** 0.5)
    diagonal = (magnitude * signs)[:, :, None]
    return jnp.where(below, scaled, 0.0) + jnp.where(on_diag, diagonal, 0.0)


def with_spikes(entries, key, source, target, parts, factor):
    def block_of(position):
        return (jnp.arange(entries.shape[position]) // (entries.shape[position] // parts)).reshape((-1,) + (1,) * (entries.ndim - 1 - position))

    one_side = jax.random.permutation(key, parts)[block_of(target)]
    far = (block_of(target) + parts // 2) % parts
    return jnp.where((block_of(source) == one_side) | (block_of(source) == far), factor * entries, entries)


def block_levels(own_key, extent, pieces, smallest, high):
    gain, own = 1.0, jax.random.fold_in(own_key, 6)
    for axis_at, parts in pieces:
        draws = jnp.exp(jax.random.uniform(jax.random.fold_in(own, axis_at), (parts,), jnp.float32, smallest / len(pieces), high / len(pieces)))
        gain = gain * jnp.repeat(draws, extent[axis_at] // parts).reshape([-1 if axis == axis_at else 1 for axis in range(len(extent))])
    return gain


def bell_draw(own_key, extent, scale, bound, cuts=(), dtype=jnp.bfloat16):
    loudness = block_levels(own_key, extent, cuts, -0.22, 0.18) if cuts else 1.0
    values = jax.random.normal(own_key, extent, jnp.float32) * scale * loudness
    return jnp.minimum(jnp.maximum(values, -bound), bound).astype(dtype)


def bell_draw_with(own_key, extent, width, bound, pieces, heavy, kind=jnp.bfloat16):
    drawn = width * jax.random.normal(own_key, extent, jnp.float32)
    if pieces:
        drawn = drawn * block_levels(own_key, extent, pieces, -0.22, 0.18)
    return jnp.clip(with_spikes(drawn, jax.random.fold_in(own_key, 3), *heavy), -bound, bound).astype(kind)


def setup_inputs(seed: int = 0) -> dict:
    key_list = jax.random.split(jax.random.key(seed), 6)
    diag_inverse = draw_diag_inverse(jax.random.fold_in(key_list[5], 71), 0)
    coupling = bell_draw(key_list[1], (BLOCK, BLOCK), BLOCK ** -0.5, 0.1875, ((0, 16), (1, 16)), jnp.float32)
    rhs_top = bell_draw(key_list[2], (2, BLOCK, ADJOINTS), 1.0, 6.0, ((1, 16),), jnp.float32)
    panel = bell_draw_with(key_list[3], (TRAIL_ROWS, 2 * BLOCK), (2 * BLOCK) ** -0.5, 0.1875, ((0, 16), (1, 16)), (1, 0, 16, 2.0), jnp.float32)
    rhs_rest = bell_draw(key_list[4], (TRAIL_ROWS, ADJOINTS), 1.0, 6.0, ((0, 256),), jnp.float32)
    return dict(diag_inverse=diag_inverse, coupling=coupling, rhs_top=rhs_top, panel=panel, rhs_rest=rhs_rest)


def product(left_side, right_side):
    return jnp.dot(left_side, right_side, precision=lax.Precision.HIGHEST, preferred_element_type=jnp.float32)


def reference(diag_inverse, coupling, rhs_top, panel, rhs_rest):
    first_solution = product(diag_inverse[0], rhs_top[0])
    remainder = rhs_top[1] - product(coupling, first_solution)
    second_solution = product(diag_inverse[1], remainder)
    adjoint_top = jnp.stack([first_solution, second_solution])
    ordered = adjoint_top.reshape(2, N_PCOL, COL_TILE, ADJOINTS).transpose(1, 0, 2, 3).reshape(2 * BLOCK, ADJOINTS)
    rhs_updated = rhs_rest - product(panel, ordered)
    return adjoint_top, rhs_updated
```

```python
import jax
import jax.numpy as jnp
from jax import lax
from jax.experimental import pallas as pl
from jax.experimental.pallas import tpu as pltpu
from jax.sharding import PartitionSpec as P

MESH = pl.DeviceIdType.MESH
F32, BF16 = jnp.float32, jnp.bfloat16


def precise(a, b):
    return jnp.dot(a, b, precision=lax.Precision.HIGHEST, preferred_element_type=F32)


def coarse(a, b):
    return jnp.dot(a, b, preferred_element_type=F32)


def remote(src, dst, send, recv, device):
    return pltpu.make_async_remote_copy(
        src_ref=src, dst_ref=dst, send_sem=send, recv_sem=recv, device_id=device, device_id_type=MESH
    )


def kernel(
    d_ref, c_ref, b_ref, p_ref, rest_ref, adj_ref, out_ref,
    d_v, c_v, b_v, p_v, pr_v, o_v, adj_v,
    cz, dm, us, ur, v1, es, er, eg, ms, mr, gx, gs, xh, xl,
    ld, st, p_s, p_r, c_s, c_r, d_s, d_r, u_s, u_r, e_s, e_r, g_s, g_r, m_s, m_r, z_s, z_r, a_s, a_r, f_s, f_r, x_s, x_r,
):
    r, c = lax.axis_index("prow"), lax.axis_index("pcol")
    x, y, z, k = r // 4, r % 4, c // 2, c % 2
    h = r % 2
    mate, twin = r + 1 - 2 * h, c + 1 - 2 * k

    def row(d):
        return (r + d) % 16

    def col(d):
        return (c + d) % 16

    def at_z(d):
        return ((z + d) % 8) * 2 + k

    def loop(low, high, body):
        def step(i, carry):
            body(i)
            return carry

        lax.fori_loop(low, high, step, 0)

    loads = [
        pltpu.make_async_copy(src, dst, ld.at[i])
        for i, (src, dst) in enumerate([(d_ref, d_v), (c_ref, c_v), (b_ref, b_v), (p_ref, p_v), (rest_ref, o_v)])
    ]
    for load in loads:
        load.start()
    pltpu.make_async_copy(p_ref.at[c], pr_v.at[c], p_r.at[0]).start()

    barrier = pltpu.get_barrier_semaphore()

    def greet(d):
        pl.semaphore_signal(barrier, inc=1, device_id=(r, col(d)), device_id_type=MESH)
        pl.semaphore_signal(barrier, inc=1, device_id=(row(d), c), device_id_type=MESH)

    loop(1, 16, greet)
    pl.semaphore_signal(barrier, inc=1, device_id=(mate, twin), device_id_type=MESH)
    for load in loads[:3]:
        load.wait()
    cz[z] = jnp.concatenate([c_v[:32], c_v[32:]], axis=1)
    dm[k] = d_v[1]
    pl.semaphore_wait(barrier, 31)

    def c_copy(d):
        return remote(cz.at[z], cz.at[z], c_s.at[d], c_r.at[d], (r, at_z(d)))

    def c_here(d):
        there = (z + 8 - d) % 8
        return remote(cz.at[there], cz.at[there], c_s.at[d], c_r.at[d], (r, at_z(d)))

    loop(1, 8, lambda d: c_copy(d).start())
    d_copy = remote(dm.at[k], dm.at[k], d_s, d_r, (r, twin))
    d_copy.start()

    loads[3].wait()

    def p_copy(d):
        return remote(p_v.at[col(d)], pr_v.at[c], p_s.at[d], p_r.at[d], (r, col(d)))

    loop(1, 16, lambda d: p_copy(d).start())

    for j in range(2):
        u = precise(d_v[j], b_v[j])
        for i in range(16):
            us[i, 32 * j : 32 * j + 32] = u[32 * (i % 2) : 32 * (i % 2) + 32, 128 * (i // 2) : 128 * (i // 2) + 128]

    def u_copy(d):
        return remote(us.at[row(d)], ur.at[d], u_s.at[d], u_r.at[d], (row(d), c))

    loop(1, 16, lambda d: u_copy(d).start())

    remote(dm.at[1 - k], dm.at[1 - k], d_s, d_r, (r, twin)).wait_recv()
    loop(1, 8, lambda d: c_here(d).wait_recv())
    upper = jnp.concatenate([cz[i][:, :64] for i in range(8)], axis=1)
    lower = jnp.concatenate([cz[i][:, 64:] for i in range(8)], axis=1)
    e = precise(dm[...].reshape(128, 64), jnp.concatenate([upper, lower], axis=0))
    for i in range(16):
        es[i] = e[32 * (i // 4) : 32 * (i // 4) + 32, 128 * (i % 4) : 128 * (i % 4) + 128]

    def e_copy(d):
        return remote(es.at[row(d)], er.at[d], e_s.at[d], e_r.at[d], (row(d), c))

    loop(1, 16, lambda d: e_copy(d).start())

    loop(1, 16, lambda d: u_copy(d).wait_recv())
    ur[0] = us[r]
    total = ur[0]
    for d in range(1, 16):
        total += ur[d]
    gx[0, x, y, z] = total[:32]
    v1[...] = total[32:]

    def z_copy(j, d):
        return remote(gx.at[j, x, y, z], gx.at[j, x, y, z], z_s.at[j, d], z_r.at[j, d], (r, at_z(d)))

    def z_here(j, d):
        there = (z + 8 - d) % 8
        return remote(gx.at[j, x, y, there], gx.at[j, x, y, there], z_s.at[j, d], z_r.at[j, d], (r, at_z(d)))

    loop(1, 8, lambda d: z_copy(0, d).start())

    loop(1, 16, lambda d: e_copy(d).wait_recv())
    er[0] = es[r]
    total = er[0]
    for d in range(1, 16):
        total += er[d]
    eg[r] = total

    def g_copy(d):
        return remote(eg.at[r], eg.at[r], g_s.at[d], g_r.at[d], (row(d), c))

    def g_here(d):
        there = (r + 16 - d) % 16
        return remote(eg.at[there], eg.at[there], g_s.at[d], g_r.at[d], (row(d), c))

    loop(1, 16, lambda d: g_copy(d).start())

    near, far = pl.ds(0, 4), pl.ds(4, 4)

    def a_copy(j, d, there=False):
        xs, ys = ((x + 4 - d) % 4, (y + 4 - d) % 4) if there else (x, y)
        one, two = gx.at[j, xs, y, near], gx.at[j, x, ys, far]
        return (
            remote(one, one, a_s.at[j, 0, d], a_r.at[j, 0, d], (((x + d) % 4) * 4 + y, c)),
            remote(two, two, a_s.at[j, 1, d], a_r.at[j, 1, d], (x * 4 + (y + d) % 4, c)),
        )

    def f_copy(j, d, there=False):
        xs, ys = ((x + 4 - d) % 4, (y + 4 - d) % 4) if there else (x, y)
        one, two = gx.at[j, :, ys, near], gx.at[j, xs, :, far]
        return (
            remote(one, one, f_s.at[j, 0, d], f_r.at[j, 0, d], (x * 4 + (y + d) % 4, c)),
            remote(two, two, f_s.at[j, 1, d], f_r.at[j, 1, d], (((x + d) % 4) * 4 + y, c)),
        )

    def start(copies):
        for copy in copies:
            copy.start()

    def arrive(copies):
        for copy in copies:
            copy.wait_recv()

    def leave(copies):
        for copy in copies:
            copy.wait_send()

    loop(1, 8, lambda d: z_here(0, d).wait_recv())
    loop(1, 4, lambda d: start(a_copy(0, d)))

    loop(1, 16, lambda d: g_here(d).wait_recv())
    e = jnp.concatenate([jnp.concatenate([eg[4 * i + j] for j in range(4)], axis=1) for i in range(4)], axis=0)
    first = h == 0
    rows = []
    for i in range(8):
        block = gx[0, x, y, i]
        rows += [jnp.where(first, block, 0.0), jnp.where(first, 0.0, block)]
    ms[...] = precise(e, jnp.concatenate(rows, axis=0)).reshape(4, 32, 128)
    others = [(1 - k, h, (r, twin)), (k, 1 - h, (mate, c)), (1 - k, 1 - h, (mate, twin))]
    m_copies = [
        remote(ms.at[2 * kk + hh], mr.at[i], m_s.at[i], m_r.at[i], device) for i, (kk, hh, device) in enumerate(others)
    ]
    start(m_copies)
    loop(1, 4, lambda d: arrive(a_copy(0, d, True)))
    loop(1, 4, lambda d: start(f_copy(0, d)))
    arrive(m_copies)
    gx[1, x, y, z] = v1[...] - (ms[2 * k + h] + mr[0] + mr[1] + mr[2])
    loop(1, 8, lambda d: z_copy(1, d).start())
    loop(1, 8, lambda d: z_here(1, d).wait_recv())
    loop(1, 4, lambda d: start(a_copy(1, d)))
    loop(1, 4, lambda d: arrive(a_copy(1, d, True)))
    loop(1, 4, lambda d: start(f_copy(1, d)))

    def x_copy(j):
        return remote(gx.at[j], gs.at[j], x_s.at[j], x_r.at[j], (r, twin))

    def split(held, j, kk):
        def body(i):
            q = 2 * i + kk
            for n in range(16):
                value = held[j, n // 4, n % 4, i]
                high = value.astype(BF16)
                rows = slice(64 * j + 32 * (n % 2), 64 * j + 32 * (n % 2) + 32)
                lanes = slice(128 * (n // 2), 128 * (n // 2) + 128)
                xh[q, rows, lanes] = high
                xl[q, rows, lanes] = (value - high.astype(F32)).astype(BF16)

        loop(0, 8, body)

    for j in range(2):
        loop(1, 4, lambda d: arrive(f_copy(j, d, True)))
        x_copy(j).start()
        split(gx, j, k)
        for n in range(16):
            adj_v[j, 32 * (n % 2) : 32 * (n % 2) + 32, 128 * (n // 2) : 128 * (n // 2) + 128] = gx[j, n // 4, n % 4, z]
        x_copy(j).wait_recv()
        split(gs, j, 1 - k)
    adj_out = pltpu.make_async_copy(adj_v, adj_ref, st.at[0])
    adj_out.start()

    loads[4].wait()

    def update(i):
        there = (z + 8 + (2 * (i % 2) - 1) * ((i + 1) // 2)) % 8
        for kk in range(2):
            q = 2 * there + kk
            d = (c + 16 - q) % 16
            remote(p_v.at[q], pr_v.at[q], p_s.at[d], p_r.at[d], (r, col(1))).wait_recv()
        block = jnp.concatenate([pr_v[2 * there], pr_v[2 * there + 1]], axis=1)
        high = block.astype(BF16)
        low = (block - high.astype(F32)).astype(BF16)
        x_high = xh[pl.ds(2 * there, 2)].reshape(256, 1024)
        x_low = xl[pl.ds(2 * there, 2)].reshape(256, 1024)
        o_v[...] -= coarse(high, x_high) + (coarse(high, x_low) + coarse(low, x_high))

    loop(0, 8, update)
    out = pltpu.make_async_copy(o_v, out_ref, st.at[1])
    out.start()

    d_copy.wait_send()
    loop(1, 8, lambda d: c_copy(d).wait_send())
    for j in range(2):
        loop(1, 8, lambda d: z_copy(j, d).wait_send())
        loop(1, 4, lambda d: leave(a_copy(j, d)))
        loop(1, 4, lambda d: leave(f_copy(j, d)))
        x_copy(j).wait_send()

    def left(d):
        p_copy(d).wait_send()
        u_copy(d).wait_send()
        e_copy(d).wait_send()
        g_copy(d).wait_send()

    loop(1, 16, left)
    leave(m_copies)
    adj_out.wait()
    out.wait()


def body(diag_inverse, coupling, rhs_top, panel, rhs_rest):
    vmem, sem = pltpu.VMEM, pltpu.SemaphoreType.DMA
    scratch = [
        vmem((2, 64, 64), F32), vmem((64, 64), F32), vmem((2, 64, 1024), F32), vmem((16, 256, 128), F32),
        vmem((16, 256, 128), F32), vmem((256, 1024), F32), vmem((2, 64, 1024), F32),
        vmem((8, 32, 128), F32), vmem((2, 64, 64), F32), vmem((16, 64, 128), F32), vmem((16, 64, 128), F32),
        vmem((32, 128), F32), vmem((16, 32, 128), F32), vmem((16, 32, 128), F32), vmem((16, 32, 128), F32),
        vmem((4, 32, 128), F32), vmem((3, 32, 128), F32),
        vmem((2, 4, 4, 8, 32, 128), F32), vmem((2, 4, 4, 8, 32, 128), F32),
        vmem((16, 128, 1024), BF16), vmem((16, 128, 1024), BF16),
        sem((5,)), sem((2,)), sem((16,)), sem((16,)), sem((8,)), sem((8,)), sem, sem,
        sem((16,)), sem((16,)), sem((16,)), sem((16,)), sem((16,)), sem((16,)), sem((3,)), sem((3,)),
        sem((2, 8)), sem((2, 8)), sem((2, 2, 4)), sem((2, 2, 4)), sem((2, 2, 4)), sem((2, 2, 4)), sem((2,)), sem((2,)),
    ]
    return pl.pallas_call(
        kernel,
        out_shape=(jax.ShapeDtypeStruct((2, 64, 1024), F32), jax.ShapeDtypeStruct((256, 1024), F32)),
        in_specs=[pl.BlockSpec(memory_space=pl.ANY)] * 5,
        out_specs=[pl.BlockSpec(memory_space=pl.ANY)] * 2,
        scratch_shapes=scratch,
        compiler_params=pltpu.CompilerParams(collective_id=0, has_side_effects=True, vmem_limit_bytes=48 * 2**20),
        name="window",
    )(diag_inverse, coupling, rhs_top, panel.reshape(16, 256, 128), rhs_rest)


def solution(mesh):
    in_specs = (
        P(None, "pcol", "prow"),
        P("prow", "pcol"),
        P(None, "prow", None),
        P("prow", "pcol"),
        P(("prow", "pcol"), None),
    )
    out_specs = (P(None, "pcol", None), P(("prow", "pcol"), None))
    return jax.shard_map(body, mesh=mesh, in_specs=in_specs, out_specs=out_specs, check_vma=False)
```

```python
import jax
import jax.numpy as jnp
from jax import lax
from jax.experimental import pallas as pl
from jax.experimental.pallas import tpu as pltpu
from jax.sharding import PartitionSpec as P

MESH = pl.DeviceIdType.MESH
F32, BF16 = jnp.float32, jnp.bfloat16


def precise(a, b):
    return jnp.dot(a, b, precision=lax.Precision.HIGHEST, preferred_element_type=F32)


def coarse(a, b):
    return jnp.dot(a, b, preferred_element_type=F32)


def remote(src, dst, send, recv, device):
    return pltpu.make_async_remote_copy(
        src_ref=src, dst_ref=dst, send_sem=send, recv_sem=recv, device_id=device, device_id_type=MESH
    )


def loop(low, high, body):
    def step(i, carry):
        body(i)
        return carry

    lax.fori_loop(low, high, step, 0)


def kernel(
    d_ref, c_ref, b_ref, p_ref, rest_ref, adj_ref, out_ref,
    d_v, c_v, b_v, p_v, pr_v, o_v, adj_v, d_t, c_t,
    cz, us, ur, v1, es, er, eg, ms, mr, gx, xh, xl,
    ld, st, p_s, p_r, h_s, h_r, d_s, d_r, c_s, c_r, u_s, u_r, e_s, e_r, g_s, g_r, m_s, m_r, z_s, z_r, n_s, n_r, f_s, f_r, x_s, x_r,
):
    r, c = lax.axis_index("prow"), lax.axis_index("pcol")
    x, y, z, k = r // 4, r % 4, c // 2, c % 2
    h = r % 2
    mate, twin = r + 1 - 2 * h, c + 1 - 2 * k
    pump, chain = k == 0, k == 1

    def row(d):
        return (r + d) % 16

    def at_z(d):
        return (z + d) % 8

    def back_z(d):
        return (z + 8 - d) % 8

    loads = [
        pltpu.make_async_copy(src, dst, ld.at[i])
        for i, (src, dst) in enumerate(
            [(d_ref, d_v), (c_ref, c_v), (b_ref, b_v), (p_ref, p_v.at[:, 0]), (rest_ref, o_v), (p_ref.at[c], pr_v.at[z, k])]
        )
    ]
    for load in loads:
        load.start()

    barrier = pltpu.get_barrier_semaphore()

    def greet(*device):
        pl.semaphore_signal(barrier, inc=1, device_id=device, device_id_type=MESH)

    greet(r, twin)
    loop(2, 16, lambda d: greet(r, (2 * z + d) % 16))

    @pl.when(chain)
    def _():
        loop(1, 16, lambda d: greet(row(d), c))

    for load in loads[:4]:
        load.wait()

    @pl.when(pump)
    def _():
        pl.semaphore_wait(barrier, 15)

    @pl.when(chain)
    def _():
        pl.semaphore_wait(barrier, 30)

    def away(i):
        return (4 + (2 * (i % 2) - 1) * ((i + 1) // 2)) % 8

    def p_copy(kk, i):
        q = 2 * at_z(away(i // 2)) + i % 2
        return remote(p_v.at[q, kk], pr_v.at[z, kk], p_s.at[kk, i], p_r.at[kk, i // 2], (r, q))

    def p_here(kk, i):
        there = back_z(away(i))
        return remote(pr_v.at[there, kk], pr_v.at[there, kk], p_s.at[kk, i], p_r.at[kk, i], (r, twin))

    def hand(i):
        q = 2 * at_z(away(i // 2)) + i % 2
        return remote(p_v.at[q, 0], p_v.at[q, 1], h_s.at[i], h_r.at[i], (r, twin))

    def swap():
        return remote(p_v.at[twin, 0], pr_v.at[z, k], h_s.at[14], h_r.at[14], (r, twin))

    def swap_here():
        return remote(p_v.at[twin, 0], pr_v.at[z, 1 - k], h_s.at[14], h_r.at[14], (r, twin))

    d_copy = remote(d_v, d_t, d_s.at[0], d_r.at[0], (r, twin))
    t_copy = remote(c_v, c_t, d_s.at[1], d_r.at[1], (r, twin))

    def c_copy(d):
        return remote(cz.at[z], cz.at[z], c_s.at[d], c_r.at[d], (r, 2 * at_z(d) + k))

    def c_here(d):
        return remote(cz.at[back_z(d)], cz.at[back_z(d)], c_s.at[d], c_r.at[d], (r, c))

    def u_copy(d):
        return remote(us.at[row(d)], ur.at[d], u_s.at[d], u_r.at[d], (row(d), c))

    def e_copy(d):
        return remote(es.at[row(d)], er.at[d], e_s.at[d], e_r.at[d], (row(d), c))

    def g_copy(d):
        return remote(eg.at[r], eg.at[r], g_s.at[d], g_r.at[d], (row(d), c))

    def g_here(d):
        return remote(eg.at[row(16 - d)], eg.at[row(16 - d)], g_s.at[d], g_r.at[d], (row(d), c))

    def z_copy(j, d):
        return remote(gx.at[j, x, y, z], gx.at[j, x, y, z], z_s.at[j, d], z_r.at[j, d], (r, 2 * at_z(d) + k))

    def z_here(j, d):
        block = gx.at[j, x, y, back_z(d)]
        return remote(block, block, z_s.at[j, d], z_r.at[j, d], (r, c))

    m_copy = remote(ms.at[1 - h], mr, m_s, m_r, (mate, c))

    near, far = pl.ds(0, 4), pl.ds(4, 4)

    def along(axis, d):
        return (((x + d) % 4) * 4 + y, c) if axis == 0 else (x * 4 + (y + d) % 4, c)

    def n_copy(j, axis, d):
        return remote(gx.at[j, x, y], gx.at[j, x, y], n_s.at[j, axis, d], n_r.at[j, axis, d], along(axis, d))

    def n_here(j, axis, d):
        block = gx.at[j, (x + 4 - d) % 4, y] if axis == 0 else gx.at[j, x, (y + 4 - d) % 4]
        return remote(block, block, n_s.at[j, axis, d], n_r.at[j, axis, d], along(axis, d))

    def f_copy(j, axis, e, d):
        block = gx.at[j, (x + 4 - e) % 4, y, near] if axis == 0 else gx.at[j, x, (y + 4 - e) % 4, far]
        return remote(block, block, f_s.at[j, axis, e, d], f_r.at[j, axis, e, d], along(1 - axis, d))

    def f_here(j, axis, e, d):
        if axis == 0:
            block = gx.at[j, (x + 4 - e) % 4, (y + 4 - d) % 4, near]
        else:
            block = gx.at[j, (x + 4 - d) % 4, (y + 4 - e) % 4, far]
        return remote(block, block, f_s.at[j, axis, e, d], f_r.at[j, axis, e, d], (r, twin))

    def x_copy(j, e, d):
        block = gx.at[j, (x + 4 - e) % 4, (y + 4 - d) % 4]
        return remote(block, block, x_s.at[j, e, d], x_r.at[j, e, d], (r, twin))

    def split(j, e, d):
        xx, yy = (x + 4 - e) % 4, (y + 4 - d) % 4
        p, hh = 2 * xx + yy // 2, yy % 2

        def body(i):
            value = gx[j, xx, yy, i]
            high = value.astype(BF16)
            xh[p, i, hh, j] = high
            xl[p, i, hh, j] = (value - high.astype(F32)).astype(BF16)

        loop(0, 8, body)

    def axes(body):
        for axis in range(2):
            loop(1, 4, lambda d: body(axis, d))

    @pl.when(pump)
    def _():
        d_copy.start()
        t_copy.start()
        swap().start()
        loop(0, 14, lambda i: p_copy(0, i).start())

        def relay(i):
            hand(i).wait_recv()
            p_copy(1, i).start()

        loop(0, 14, relay)
        for j in range(2):

            def take(i):
                x_copy(j, i // 4, i % 4).wait_recv()
                split(j, i // 4, i % 4)

            loop(0, 16, take)

    @pl.when(chain)
    def _():
        t_copy.wait_recv()
        cz[z] = jnp.concatenate([c_t[...], c_v[...]], axis=1)
        loop(1, 8, lambda d: c_copy(d).start())

        d_copy.wait_recv()
        for j in range(2):
            for i, part in enumerate((d_t, d_v)):
                u = precise(part[j], b_v[j])
                for n in range(8):
                    us[2 * n + i, j] = u[:, 128 * n : 128 * n + 128]
        loop(1, 16, lambda d: u_copy(d).start())
        swap().start()
        loop(0, 14, lambda i: hand(i).start())

        loop(1, 8, lambda d: c_here(d).wait_recv())
        both = jnp.concatenate([d_t[1], d_v[1]], axis=0)
        for n in range(8):
            e = precise(both, cz[n])
            es[n] = e[:64]
            es[8 + n] = e[64:]
        loop(1, 16, lambda d: e_copy(d).start())

        loop(1, 16, lambda d: u_copy(d).wait_recv())
        ur[0] = us[r]
        gx[0, x, y, z] = sum(ur[d, 0] for d in range(16))
        loop(1, 8, lambda d: z_copy(0, d).start())
        v1[...] = sum(ur[d, 1] for d in range(16))

        loop(1, 16, lambda d: e_copy(d).wait_recv())
        er[0] = es[r]
        eg[r] = sum(er[d] for d in range(16))
        loop(1, 16, lambda d: g_copy(d).start())

        loop(1, 8, lambda d: z_here(0, d).wait_recv())
        axes(lambda axis, d: n_copy(0, axis, d).start())

        loop(1, 16, lambda d: g_here(d).wait_recv())
        first = h == 0
        wide = []
        for i in range(8):
            block = gx[0, x, y, i]
            wide += [jnp.where(first, block, 0.0), jnp.where(first, 0.0, block)]
        wide = jnp.concatenate(wide, axis=0)
        for i in range(2):
            ms[i] = precise(jnp.concatenate([eg[8 * i + n] for n in range(8)], axis=1), wide)
        m_copy.start()
        m_copy.wait_recv()
        gx[1, x, y, z] = v1[...] - (ms[h] + mr[...])
        loop(1, 8, lambda d: z_copy(1, d).start())

        def forward(j):
            def body(axis, e):
                n_here(j, axis, e).wait_recv()
                loop(1, 4, lambda d: f_copy(j, axis, e, d).start())

            axes(body)

        def cross(j):
            def body(i):
                e, d = i // 4, i % 4

                @pl.when((e > 0) & (d > 0))
                def _():
                    f_here(j, 0, e, d).wait_recv()
                    f_here(j, 1, d, e).wait_recv()

                x_copy(j, e, d).start()
                split(j, e, d)

            loop(0, 16, body)

        forward(0)
        loop(1, 8, lambda d: z_here(1, d).wait_recv())
        axes(lambda axis, d: n_copy(1, axis, d).start())
        cross(0)
        forward(1)
        cross(1)

    for n in range(8):
        for j in range(2):
            adj_v[j, :, 128 * n : 128 * n + 128] = gx[j, n // 2, 2 * (n % 2) + k, z]
    adj_out = pltpu.make_async_copy(adj_v, adj_ref, st.at[0])
    adj_out.start()

    loads[4].wait()
    loads[5].wait()
    swap_here().wait_recv()

    def update(there):
        block = jnp.concatenate([pr_v[there, 0], pr_v[there, 1]], axis=1)
        high = block.astype(BF16)
        low = (block - high.astype(F32)).astype(BF16)
        x_high = jnp.concatenate([xh[n, there].reshape(256, 128) for n in range(8)], axis=1)
        x_low = jnp.concatenate([xl[n, there].reshape(256, 128) for n in range(8)], axis=1)
        o_v[...] -= coarse(high, x_high) + (coarse(high, x_low) + coarse(low, x_high))

    def step(i):
        @pl.when(i > 0)
        def _():
            p_here(0, i - 1).wait_recv()
            p_here(1, i - 1).wait_recv()

        update(jnp.where(i == 0, z, back_z(away(i - 1))))

    loop(0, 8, step)
    out = pltpu.make_async_copy(o_v, out_ref, st.at[1])
    out.start()

    swap().wait_send()

    @pl.when(pump)
    def _():
        d_copy.wait_send()
        t_copy.wait_send()

        def left(i):
            p_copy(0, i).wait_send()
            p_copy(1, i).wait_send()

        loop(0, 14, left)

    @pl.when(chain)
    def _():
        loop(0, 14, lambda i: hand(i).wait_send())
        loop(1, 8, lambda d: c_copy(d).wait_send())

        def left(d):
            u_copy(d).wait_send()
            e_copy(d).wait_send()
            g_copy(d).wait_send()

        loop(1, 16, left)
        m_copy.wait_send()
        for j in range(2):
            loop(1, 8, lambda d: z_copy(j, d).wait_send())
            loop(0, 16, lambda i: x_copy(j, i // 4, i % 4).wait_send())

            def left(axis, e):
                n_copy(j, axis, e).wait_send()
                loop(1, 4, lambda d: f_copy(j, axis, e, d).wait_send())

            axes(left)

    adj_out.wait()
    out.wait()


def body(diag_inverse, coupling, rhs_top, panel, rhs_rest):
    vmem, sem = pltpu.VMEM, pltpu.SemaphoreType.DMA
    scratch = [
        vmem((2, 64, 64), F32), vmem((64, 64), F32), vmem((2, 64, 1024), F32), vmem((16, 2, 256, 128), F32),
        vmem((8, 2, 256, 128), F32), vmem((256, 1024), F32), vmem((2, 64, 1024), F32), vmem((2, 64, 64), F32), vmem((64, 64), F32),
        vmem((8, 64, 128), F32), vmem((16, 2, 64, 128), F32), vmem((16, 2, 64, 128), F32), vmem((64, 128), F32),
        vmem((16, 64, 128), F32), vmem((16, 64, 128), F32), vmem((16, 64, 128), F32), vmem((2, 64, 128), F32), vmem((64, 128), F32),
        vmem((2, 4, 4, 8, 64, 128), F32), vmem((8, 8, 2, 2, 64, 128), BF16), vmem((8, 8, 2, 2, 64, 128), BF16),
        sem((6,)), sem((2,)), sem((2, 14)), sem((2, 7)), sem((15,)), sem((15,)), sem((2,)), sem((2,)), sem((8,)), sem((8,)),
        sem((16,)), sem((16,)), sem((16,)), sem((16,)), sem((16,)), sem((16,)), sem, sem, sem((2, 8)), sem((2, 8)),
        sem((2, 2, 4)), sem((2, 2, 4)), sem((2, 2, 4, 4)), sem((2, 2, 4, 4)), sem((2, 4, 4)), sem((2, 4, 4)),
    ]
    return pl.pallas_call(
        kernel,
        out_shape=(jax.ShapeDtypeStruct((2, 64, 1024), F32), jax.ShapeDtypeStruct((256, 1024), F32)),
        in_specs=[pl.BlockSpec(memory_space=pl.ANY)] * 5,
        out_specs=[pl.BlockSpec(memory_space=pl.ANY)] * 2,
        scratch_shapes=scratch,
        compiler_params=pltpu.CompilerParams(collective_id=0, has_side_effects=True, vmem_limit_bytes=60 * 2**20),
        name="window",
    )(diag_inverse, coupling, rhs_top, panel.reshape(16, 256, 128), rhs_rest)


def solution(mesh):
    in_specs = (
        P(None, "pcol", "prow"),
        P("prow", "pcol"),
        P(None, "prow", None),
        P("prow", "pcol"),
        P(("prow", "pcol"), None),
    )
    out_specs = (P(None, "pcol", None), P(("prow", "pcol"), None))
    return jax.shard_map(body, mesh=mesh, in_specs=in_specs, out_specs=out_specs, check_vma=False)
```

```python
import jax
import jax.numpy as jnp
from jax import lax
from jax.experimental import pallas as pl
from jax.experimental.pallas import tpu as pltpu
from jax.sharding import PartitionSpec as P

MESH = pl.DeviceIdType.MESH
F32, BF16 = jnp.float32, jnp.bfloat16


def precise(a, b):
    return jnp.dot(a, b, precision=lax.Precision.HIGHEST, preferred_element_type=F32)


def coarse(a, b):
    return jnp.dot(a, b, preferred_element_type=F32)


def remote(src, dst, send, recv, device):
    return pltpu.make_async_remote_copy(
        src_ref=src, dst_ref=dst, send_sem=send, recv_sem=recv, device_id=device, device_id_type=MESH
    )


def loop(low, high, body):
    def step(i, carry):
        body(i)
        return carry

    lax.fori_loop(low, high, step, 0)


def kernel(
    d_ref, c_ref, b_ref, p_ref, rest_ref, adj_ref, out_ref,
    d_v, c_v, b_v, p_v, pr_v, o_v, adj_v, d_t,
    cz, us, ur, es, er, eg, gx, xh, xl,
    ld, st, p_s, p_r, h_s, h_r, d_s, d_r, c_s, c_r, u_s, u_r, e_s, e_r, g_s, g_r, z_s, z_r, n_s, n_r, o_s, o_r, f_s, f_r, x_s, x_r,
):
    r, c = lax.axis_index("prow"), lax.axis_index("pcol")
    x, y, z, k = r // 4, r % 4, c // 2, c % 2
    h = r % 2
    twin = c + 1 - 2 * k
    pump, chain = k == 0, k == 1

    def row(d):
        return (r + d) % 16

    def at_z(d):
        return (z + d) % 8

    def back_z(d):
        return (z + 8 - d) % 8

    loads = [
        pltpu.make_async_copy(src, dst, ld.at[i])
        for i, (src, dst) in enumerate(
            [(d_ref, d_v), (c_ref, c_v), (b_ref, b_v), (p_ref, p_v.at[:, 0]), (rest_ref, o_v), (p_ref.at[c], pr_v.at[z, k])]
        )
    ]
    for load in loads:
        load.start()

    barrier = pltpu.get_barrier_semaphore()

    def greet(*device):
        pl.semaphore_signal(barrier, inc=1, device_id=device, device_id_type=MESH)

    greet(r, twin)
    loop(2, 16, lambda d: greet(r, (2 * z + d) % 16))

    loop(1, 16, lambda d: greet(row(d), c))

    @pl.when(chain & (h == 0))
    def _():
        loop(1, 16, lambda d: greet(row(d), twin))

    @pl.when(chain & (h == 1))
    def _():
        loop(1, 8, lambda d: greet(row(2 * d), twin))

    for load in loads[:3]:
        load.wait()
    for j in range(2):
        u = precise(d_v[j], b_v[j])
        for n in range(8):
            us[j, n] = u[:, 128 * n : 128 * n + 128]
    cz[z, k] = jnp.concatenate([c_v[:32], c_v[32:]], axis=1)

    @pl.when(chain & (h == 1))
    def _():
        for j in range(2):
            ur[j, r] = us[j, r // 2]

    loads[3].wait()

    @pl.when(pump)
    def _():
        pl.semaphore_wait(barrier, 37 + 8 * h)

    @pl.when(chain)
    def _():
        pl.semaphore_wait(barrier, 30)

    def away(i):
        return (4 + (2 * (i % 2) - 1) * ((i + 1) // 2)) % 8

    def p_copy(kk, i):
        q = 2 * at_z(away(i // 2)) + i % 2
        return remote(p_v.at[q, kk], pr_v.at[z, kk], p_s.at[kk, i], p_r.at[kk, i // 2], (r, q))

    def p_here(kk, i):
        there = back_z(away(i))
        return remote(pr_v.at[there, kk], pr_v.at[there, kk], p_s.at[kk, i], p_r.at[kk, i], (r, twin))

    def hand(i):
        q = 2 * at_z(away(i // 2)) + i % 2
        return remote(p_v.at[q, 0], p_v.at[q, 1], h_s.at[i], h_r.at[i], (r, twin))

    def swap():
        return remote(p_v.at[twin, 0], pr_v.at[z, k], h_s.at[14], h_r.at[14], (r, twin))

    def swap_here():
        return remote(p_v.at[twin, 0], pr_v.at[z, 1 - k], h_s.at[14], h_r.at[14], (r, twin))

    d_copy = remote(d_v.at[1], d_t, d_s, d_r, (r, twin))

    def c_copy(d):
        return remote(cz.at[z, k], cz.at[z, k], c_s.at[d], c_r.at[k, d], (r, 2 * at_z(d)))

    def c_here(kk, d):
        block = cz.at[back_z(d), kk]
        return remote(block, block, c_s.at[d], c_r.at[kk, d], (r, twin))

    def u_copy(j, n):
        return remote(us.at[j, n], ur.at[j, r], u_s.at[j, n], u_r.at[j, r], (2 * n + k, 2 * z + 1))

    def u_here(j, i):
        return remote(us.at[j, 0], ur.at[j, i], u_s.at[j, 0], u_r.at[j, i], (r, twin))

    def unless_own(n, body):
        @pl.when(pump | (2 * n + 1 != r))
        def _():
            body()

    def u_send(j):
        loop(0, 8, lambda n: unless_own(n, lambda: u_copy(j, n).start()))

    def u_sent(j):
        loop(0, 8, lambda n: unless_own(n, lambda: u_copy(j, n).wait_send()))

    def u_arrive(j):
        def body(i):
            @pl.when((h == 0) | (i != r))
            def _():
                u_here(j, i).wait_recv()

        loop(0, 16, body)

    def e_copy(d):
        return remote(es.at[row(d)], er.at[d], e_s.at[d], e_r.at[d], (row(d), c))

    def g_copy(d):
        return remote(eg.at[r // 2], eg.at[r // 2], g_s.at[d], g_r.at[d], (row(2 * d), 2 * z + 1))

    def g_here(d):
        block = eg.at[row(16 - 2 * d) // 2]
        return remote(block, block, g_s.at[d], g_r.at[d], (r, twin))

    def z_copy(j, d):
        block = gx.at[j, x, y, z // 2, z % 2]
        return remote(block, block, z_s.at[j, d], z_r.at[j, d], (r, 2 * at_z(d) + k))

    def z_here(j, d):
        block = gx.at[j, x, y, back_z(d) // 2, back_z(d) % 2]
        return remote(block, block, z_s.at[j, d], z_r.at[j, d], (r, c))

    def along(axis, d):
        return (((x + d) % 4) * 4 + y, c) if axis == 0 else (x * 4 + (y + d) % 4, c)

    def n_copy(j, axis, d, i, a, on):
        block = gx.at[j, x, y, i, a]
        if on:
            return remote(block, block, n_s.at[j, axis, d, i], n_r.at[j, axis, d, i], along(axis, d))
        return remote(block, block, o_s.at[j, axis, d], o_r.at[j, axis, d], along(axis, d))

    def n_here(j, a, d, i):
        block = gx.at[j, (x + 4 - (1 - a) * d) % 4, (y + 4 - a * d) % 4, i, a]
        return remote(block, block, n_s.at[j, a, d, i], n_r.at[j, a, d, i], (r, twin))

    def o_all(j, axis, d, here):
        xx, yy = x, y
        if here:
            xx, yy = ((x + 4 - d) % 4, y) if axis == 0 else (x, (y + 4 - d) % 4)
        block = gx.at[j, xx, yy, :, 1 - axis]
        return remote(block, block, o_s.at[j, axis, d], o_r.at[j, axis, d], (r, twin))

    def f_copy(j, a, e, d, i):
        block = gx.at[j, (x + 4 - (1 - a) * e) % 4, (y + 4 - a * e) % 4, i, a]
        to = ((x + a * d) % 4) * 4 + (y + (1 - a) * d) % 4
        return remote(block, block, f_s.at[j, a, e, d], f_r.at[j, a, e, d], (to, c))

    def f_all(j, a, e, d):
        block = gx.at[j, (x + 4 - (1 - a) * e - a * d) % 4, (y + 4 - a * e - (1 - a) * d) % 4, :, a]
        return remote(block, block, f_s.at[j, a, e, d], f_r.at[j, a, e, d], (r, twin))

    def x_copy(j, e, d):
        block = gx.at[j, (x + 4 - e) % 4, (y + 4 - d) % 4]
        return remote(block, block, x_s.at[j, e, d], x_r.at[j, e, d], (r, twin))

    def split(j, e, d):
        xx, yy = (x + 4 - e) % 4, (y + 4 - d) % 4
        p, hh = 2 * xx + yy // 2, yy % 2

        def body(i):
            value = gx[j, xx, yy, i // 2, i % 2]
            high = value.astype(BF16)
            xh[p, i, hh, j] = high
            xl[p, i, hh, j] = (value - high.astype(F32)).astype(BF16)

        loop(0, 8, body)

    def side(i):
        return ((2 * (i % 2) - 1) * ((i + 1) // 2) + 8) % 8

    def spread(j):
        def body(i):
            @pl.when(i > 0)
            def _():
                z_here(j, side(i)).wait_recv()

            piece = back_z(side(i))
            for a in range(2):

                @pl.when(piece % 2 == a)
                def _():
                    for axis in (a, 1 - a):
                        for d in (1, 3, 2):
                            n_copy(j, axis, d, piece // 2, a, axis == a).start()

        loop(0, 8, body)

    def forward(j):
        def body(i):
            piece = back_z(side(i))
            for e in (1, 3, 2):
                n_here(j, piece % 2, e, piece // 2).wait_recv()
                for d in (1, 3, 2):
                    f_copy(j, piece % 2, e, d, piece // 2).start()

        loop(0, 8, body)
        for axis in range(2):
            loop(1, 4, lambda d: o_all(j, axis, d, True).wait_recv())

    def cross(j):
        def body(i):
            e, d = i // 4, i % 4

            @pl.when((e > 0) & (d > 0))
            def _():
                f_all(j, 0, e, d).wait_recv()
                f_all(j, 1, d, e).wait_recv()

            x_copy(j, e, d).start()
            split(j, e, d)

        loop(0, 16, body)

    @pl.when(pump)
    def _():
        loop(1, 8, lambda d: c_copy(d).start())
        u_send(0)
        loop(0, 14, lambda i: p_copy(0, i).start())
        swap().start()

        d_copy.wait_recv()
        c_here(1, 0).wait_recv()

        def both_here(d):
            c_here(0, d).wait_recv()
            c_here(1, d).wait_recv()

        loop(1, 8, both_here)
        both = jnp.concatenate([d_v[1], d_t[...]], axis=0)
        for n in range(8):
            upper = jnp.concatenate([cz[n, 0][:, :64], cz[n, 1][:, :64]], axis=1)
            lower = jnp.concatenate([cz[n, 0][:, 64:], cz[n, 1][:, 64:]], axis=1)
            e = precise(both, jnp.concatenate([upper, lower], axis=0))
            es[2 * n] = e[:64]
            es[2 * n + 1] = e[64:]
        loop(1, 16, lambda d: e_copy(d).start())
        u_send(1)

        def relay(i):
            hand(i).wait_recv()
            p_copy(1, i).start()

        loop(0, 14, relay)

        loop(1, 16, lambda d: e_copy(d).wait_recv())
        er[0] = es[r]
        eg[r // 2] = sum(er[d] for d in range(16))
        loop(0, 8, lambda d: g_copy(d).start())

        for j in range(2):

            def take(i):
                x_copy(j, i // 4, i % 4).wait_recv()
                split(j, i // 4, i % 4)

            loop(0, 16, take)

    @pl.when(chain)
    def _():
        u_send(0)
        loop(0, 8, lambda d: c_copy(d).start())
        d_copy.start()
        swap().start()
        loop(0, 14, lambda i: hand(i).start())

        u_arrive(0)
        gx[0, x, y, z // 2, z % 2] = sum(ur[0, i] for i in range(16))
        loop(1, 8, lambda d: z_copy(0, d).start())
        u_send(1)
        spread(0)
        forward(0)

        u_arrive(1)
        total = sum(ur[1, i] for i in range(16))
        tile = [gx[0, x, 2 * (y // 2) + hh, n // 2, n % 2] for n in range(8) for hh in range(2)]
        loop(0, 8, lambda d: g_here(d).wait_recv())
        e = jnp.concatenate([eg[n] for n in range(8)], axis=1)
        gx[1, x, y, z // 2, z % 2] = total - precise(e, jnp.concatenate(tile, axis=0))
        loop(1, 8, lambda d: z_copy(1, d).start())
        spread(1)
        cross(0)
        forward(1)
        cross(1)

    for n in range(8):
        for j in range(2):
            adj_v[j, :, 128 * n : 128 * n + 128] = gx[j, n // 2, 2 * (n % 2) + k, z // 2, z % 2]
    adj_out = pltpu.make_async_copy(adj_v, adj_ref, st.at[0])
    adj_out.start()

    loads[4].wait()
    loads[5].wait()
    swap_here().wait_recv()

    def update(there):
        block = jnp.concatenate([pr_v[there, 0], pr_v[there, 1]], axis=1)
        high = block.astype(BF16)
        low = (block - high.astype(F32)).astype(BF16)
        both = jnp.concatenate([high, low], axis=0)
        for n in range(4):
            x_high = jnp.concatenate([xh[2 * n + i, there].reshape(256, 128) for i in range(2)], axis=1)
            x_low = jnp.concatenate([xl[2 * n + i, there].reshape(256, 128) for i in range(2)], axis=1)
            one, two = coarse(both, x_high), coarse(high, x_low)
            o_v[:, 256 * n : 256 * n + 256] -= one[:256] + (two + one[256:])

    def step(i):
        @pl.when(i > 0)
        def _():
            p_here(0, i - 1).wait_recv()
            p_here(1, i - 1).wait_recv()

        update(jnp.where(i == 0, z, back_z(away(i - 1))))

    loop(0, 8, step)
    out = pltpu.make_async_copy(o_v, out_ref, st.at[1])
    out.start()

    swap().wait_send()
    loop(1, 8, lambda d: c_copy(d).wait_send())
    for j in range(2):
        u_sent(j)

    @pl.when(pump)
    def _():
        def left(i):
            p_copy(0, i).wait_send()
            p_copy(1, i).wait_send()

        loop(0, 14, left)
        loop(1, 16, lambda d: e_copy(d).wait_send())
        loop(0, 8, lambda d: g_copy(d).wait_send())

    @pl.when(chain)
    def _():
        d_copy.wait_send()
        c_copy(0).wait_send()
        loop(0, 14, lambda i: hand(i).wait_send())
        for j in range(2):
            loop(1, 8, lambda d: z_copy(j, d).wait_send())
            loop(0, 16, lambda i: x_copy(j, i // 4, i % 4).wait_send())
            for axis in range(2):

                def left(e):
                    o_all(j, axis, e, False).wait_send()
                    loop(0, 4, lambda i: n_copy(j, axis, e, i, axis, True).wait_send())
                    loop(1, 4, lambda d: f_all(j, axis, e, d).wait_send())

                loop(1, 4, left)

    adj_out.wait()
    out.wait()


def body(diag_inverse, coupling, rhs_top, panel, rhs_rest):
    vmem, sem = pltpu.VMEM, pltpu.SemaphoreType.DMA
    scratch = [
        vmem((2, 64, 64), F32), vmem((64, 64), F32), vmem((2, 64, 1024), F32), vmem((16, 2, 256, 128), F32),
        vmem((8, 2, 256, 128), F32), vmem((256, 1024), F32), vmem((2, 64, 1024), F32), vmem((64, 64), F32),
        vmem((8, 2, 32, 128), F32), vmem((2, 8, 64, 128), F32), vmem((2, 16, 64, 128), F32),
        vmem((16, 64, 128), F32), vmem((16, 64, 128), F32), vmem((8, 64, 128), F32),
        vmem((2, 4, 4, 4, 2, 64, 128), F32), vmem((8, 8, 2, 2, 64, 128), BF16), vmem((8, 8, 2, 2, 64, 128), BF16),
        sem((6,)), sem((2,)), sem((2, 14)), sem((2, 7)), sem((15,)), sem((15,)), sem, sem, sem((8,)), sem((2, 8)),
        sem((2, 8)), sem((2, 16)), sem((16,)), sem((16,)), sem((8,)), sem((8,)), sem((2, 8)), sem((2, 8)),
        sem((2, 2, 4, 4)), sem((2, 2, 4, 4)), sem((2, 2, 4)), sem((2, 2, 4)), sem((2, 2, 4, 4)), sem((2, 2, 4, 4)), sem((2, 4, 4)), sem((2, 4, 4)),
    ]
    return pl.pallas_call(
        kernel,
        out_shape=(jax.ShapeDtypeStruct((2, 64, 1024), F32), jax.ShapeDtypeStruct((256, 1024), F32)),
        in_specs=[pl.BlockSpec(memory_space=pl.ANY)] * 5,
        out_specs=[pl.BlockSpec(memory_space=pl.ANY)] * 2,
        scratch_shapes=scratch,
        compiler_params=pltpu.CompilerParams(collective_id=0, has_side_effects=True, vmem_limit_bytes=60 * 2**20),
        name="window",
    )(diag_inverse, coupling, rhs_top, panel.reshape(16, 256, 128), rhs_rest)


def solution(mesh):
    in_specs = (
        P(None, "pcol", "prow"),
        P("prow", "pcol"),
        P(None, "prow", None),
        P("prow", "pcol"),
        P(("prow", "pcol"), None),
    )
    out_specs = (P(None, "pcol", None), P(("prow", "pcol"), None))
    return jax.shard_map(body, mesh=mesh, in_specs=in_specs, out_specs=out_specs, check_vma=False)
```

```python
import jax
import jax.numpy as jnp
from jax import lax
from jax.experimental import pallas as pl
from jax.experimental.pallas import tpu as pltpu
from jax.sharding import PartitionSpec as P

MESH = pl.DeviceIdType.MESH
F32, BF16 = jnp.float32, jnp.bfloat16


def precise(a, b):
    return jnp.dot(a, b, precision=lax.Precision.HIGHEST, preferred_element_type=F32)


def coarse(a, b):
    return jnp.dot(a, b, preferred_element_type=F32)


def remote(src, dst, send, recv, device):
    return pltpu.make_async_remote_copy(
        src_ref=src, dst_ref=dst, send_sem=send, recv_sem=recv, device_id=device, device_id_type=MESH
    )


def loop(low, high, body):
    def step(i, carry):
        body(i)
        return carry

    lax.fori_loop(low, high, step, 0)


def kernel(
    d_ref, c_ref, b_ref, p_ref, rest_ref, adj_ref, out_ref,
    d_v, c_v, b_v, p_v, pr_v, o_v, adj_v, d_t,
    cz, us, ur, es, er, eg, gx, xh, xl,
    ld, st, p_s, p_r, h_s, h_r, w_s, w_r, d_s, d_r, c_s, c_r, u_s, u_r, e_s, e_r, g_s, g_r, z_s, z_r, n_s, n_r, o_r, f_s, f_r, x_s, x_r,
):
    r, c = lax.axis_index("prow"), lax.axis_index("pcol")
    x, y, z, k = r // 4, r % 4, c // 2, c % 2
    h = r % 2
    twin = c + 1 - 2 * k
    pump, chain = k == 0, k == 1

    def row(d):
        return (r + d) % 16

    def at_z(d):
        return (z + d) % 8

    def back_z(d):
        return (z + 8 - d) % 8

    loads = [
        pltpu.make_async_copy(src, dst, ld.at[i])
        for i, (src, dst) in enumerate(
            [(d_ref, d_v), (c_ref, c_v), (b_ref, b_v), (p_ref, p_v.at[:, 0]), (rest_ref, o_v), (p_ref.at[c], pr_v.at[z, k])]
        )
    ]
    for load in loads:
        load.start()

    barrier = pltpu.get_barrier_semaphore()

    def greet(*device):
        pl.semaphore_signal(barrier, inc=1, device_id=device, device_id_type=MESH)

    greet(r, twin)
    loop(2, 16, lambda d: greet(r, (2 * z + d) % 16))

    loop(1, 16, lambda d: greet(row(d), c))

    @pl.when(chain & (h == 0))
    def _():
        loop(1, 16, lambda d: greet(row(d), twin))

    @pl.when(chain & (h == 1))
    def _():
        loop(1, 8, lambda d: greet(row(2 * d), twin))

    for load in loads[:3]:
        load.wait()
    for j in range(2):
        u = precise(d_v[j], b_v[j])
        for n in range(8):
            us[j, n] = u[:, 128 * n : 128 * n + 128]
    cz[c] = jnp.concatenate([c_v[:32], c_v[32:]], axis=1)

    @pl.when(chain & (h == 1))
    def _():
        for j in range(2):
            pltpu.make_async_copy(us.at[j, r // 2], ur.at[j, r], u_r.at[j]).start()

    loads[3].wait()

    @pl.when(pump)
    def _():
        pl.semaphore_wait(barrier, 37 + 8 * h)

    @pl.when(chain)
    def _():
        pl.semaphore_wait(barrier, 30)

    def away(i):
        return (4 + (2 * (i % 2) - 1) * ((i + 1) // 2)) % 8

    def p_copy(kk, i):
        q = 2 * at_z(away(i // 2)) + i % 2
        return remote(p_v.at[q, kk], pr_v.at[z, kk], p_s, p_r.at[i // 2], (r, q))

    def p_here(i):
        block = pr_v.at[back_z(away(i))]
        return remote(block, block, p_s, p_r.at[i], (r, twin))

    def hand(i):
        q = 2 * at_z(away(i // 2)) + i % 2
        return remote(p_v.at[q, 0], p_v.at[q, 1], h_s, h_r, (r, twin))

    def swap():
        return remote(p_v.at[twin, 0], pr_v.at[z, k], w_s, w_r, (r, twin))

    def group(block, sem):
        return remote(block, block, sem, sem, (r, twin))

    d_copy = remote(d_v.at[1], d_t, d_s, d_r, (r, twin))

    def c_copy(d):
        return remote(cz.at[c], cz.at[c], c_s, c_r, (r, 2 * at_z(d)))

    def u_send(j):
        def body(n):
            @pl.when(pump | (2 * n + 1 != r))
            def _():
                remote(us.at[j, n], ur.at[j, r], u_s, u_r.at[j], (2 * n + k, 2 * z + 1)).start()

        loop(0, 8, body)

    def e_copy(d):
        return remote(es.at[row(d)], er.at[d], e_s, e_r, (row(d), c))

    def g_copy(d):
        return remote(eg.at[r // 2], eg.at[r // 2], g_s, g_r, (row(2 * d), 2 * z + 1))

    def z_copy(j, d):
        block = gx.at[j, x, y, z // 2, z % 2]
        return remote(block, block, z_s, z_r.at[j, d], (r, 2 * at_z(d) + k))

    def z_here(j, d):
        block = gx.at[j, x, y, back_z(d) // 2, back_z(d) % 2]
        return remote(block, block, z_s, z_r.at[j, d], (r, c))

    def along(axis, d):
        return (((x + d) % 4) * 4 + y, c) if axis == 0 else (x * 4 + (y + d) % 4, c)

    def n_copy(j, axis, d, i, a):
        block = gx.at[j, x, y, i, a]
        return remote(block, block, n_s, n_r.at[j, i, a] if axis == a else o_r.at[j], along(axis, d))

    def f_copy(j, a, e, d, i):
        block = gx.at[j, (x + 4 - (1 - a) * e) % 4, (y + 4 - a * e) % 4, i, a]
        to = ((x + a * d) % 4) * 4 + (y + (1 - a) * d) % 4
        return remote(block, block, f_s.at[j], f_r.at[j, (1 - a) * e + a * d], (to, c))

    def x_copy(j, e):
        block = gx.at[j, (x + 4 - e) % 4]
        return remote(block, block, x_s.at[j], x_r.at[j, e], (r, twin))

    def split(j, e, d):
        xx, yy = (x + 4 - e) % 4, (y + 4 - d) % 4
        p, hh = 2 * xx + yy // 2, yy % 2

        def body(i):
            value = gx[j, xx, yy, i // 2, i % 2]
            high = value.astype(BF16)
            xh[p, i, hh, j] = high
            xl[p, i, hh, j] = (value - high.astype(F32)).astype(BF16)

        loop(0, 8, body)

    def side(i):
        return ((2 * (i % 2) - 1) * ((i + 1) // 2) + 8) % 8

    def spread(j):
        def body(i):
            @pl.when(i > 0)
            def _():
                z_here(j, side(i)).wait_recv()

            piece = back_z(side(i))
            for a in range(2):

                @pl.when(piece % 2 == a)
                def _():
                    for axis in (a, 1 - a):
                        for d in (1, 3, 2):
                            n_copy(j, axis, d, piece // 2, a).start()

        loop(0, 8, body)

    def forward(j):
        def body(i):
            piece = back_z(side(i))
            n, a = piece // 2, piece % 2
            group(gx.at[j, 0:3, y, n, a], n_r.at[j, n, a]).wait_recv()
            for e in (1, 3, 2):
                for d in (1, 3, 2):
                    f_copy(j, a, e, d, n).start()

        loop(0, 8, body)
        group(gx.at[j, 0:3, 0], o_r.at[j]).wait_recv()

    def take(j, e):
        loop(0, 4, lambda d: split(j, e, d))

    def cross(j):
        for e in (0, 1, 3, 2):
            if e:
                group(gx.at[j, x, 0:3], f_r.at[j, e]).wait_recv()
            x_copy(j, e).start()
            take(j, e)

    @pl.when(pump)
    def _():
        loop(1, 8, lambda d: c_copy(d).start())
        u_send(0)
        loop(0, 14, lambda i: p_copy(0, i).start())
        swap().start()

        d_copy.wait_recv()
        group(cz.at[0:15], c_r).wait_recv()
        both = jnp.concatenate([d_v[1], d_t[...]], axis=0)
        for n in range(8):
            upper = jnp.concatenate([cz[2 * n][:, :64], cz[2 * n + 1][:, :64]], axis=1)
            lower = jnp.concatenate([cz[2 * n][:, 64:], cz[2 * n + 1][:, 64:]], axis=1)
            e = precise(both, jnp.concatenate([upper, lower], axis=0))
            es[2 * n] = e[:64]
            es[2 * n + 1] = e[64:]
        loop(1, 16, lambda d: e_copy(d).start())
        u_send(1)

        group(p_v.at[0:7], h_r).wait_recv()
        loop(0, 14, lambda i: p_copy(1, i).start())

        group(er.at[1:16], e_r).wait_recv()
        er[0] = es[r]
        eg[r // 2] = sum(er[d] for d in range(16))
        loop(0, 8, lambda d: g_copy(d).start())

        for j in range(2):
            for e in (0, 1, 3, 2):
                x_copy(j, e).wait_recv()
                take(j, e)

    @pl.when(chain)
    def _():
        u_send(0)
        loop(0, 8, lambda d: c_copy(d).start())
        d_copy.start()
        swap().start()
        loop(0, 14, lambda i: hand(i).start())

        group(ur.at[0], u_r.at[0]).wait_recv()
        gx[0, x, y, z // 2, z % 2] = sum(ur[0, i] for i in range(16))
        loop(1, 8, lambda d: z_copy(0, d).start())
        u_send(1)
        spread(0)
        forward(0)

        group(ur.at[1], u_r.at[1]).wait_recv()
        total = sum(ur[1, i] for i in range(16))
        tile = [gx[0, x, 2 * (y // 2) + hh, n // 2, n % 2] for n in range(8) for hh in range(2)]
        group(eg, g_r).wait_recv()
        e = jnp.concatenate([eg[n] for n in range(8)], axis=1)
        gx[1, x, y, z // 2, z % 2] = total - precise(e, jnp.concatenate(tile, axis=0))
        loop(1, 8, lambda d: z_copy(1, d).start())
        spread(1)
        cross(0)
        forward(1)
        cross(1)

    for n in range(8):
        for j in range(2):
            adj_v[j, :, 128 * n : 128 * n + 128] = gx[j, n // 2, 2 * (n % 2) + k, z // 2, z % 2]
    adj_out = pltpu.make_async_copy(adj_v, adj_ref, st.at[0])
    adj_out.start()

    swap().wait_send()

    @pl.when(pump)
    def _():
        group(cz.at[0:7], c_s).wait_send()
        group(us, u_s).wait_send()
        group(es.at[0:15], e_s).wait_send()
        group(eg, g_s).wait_send()

    @pl.when(chain)
    def _():
        group(cz.at[0:8], c_s).wait_send()

        @pl.when(h == 0)
        def _():
            group(us, u_s).wait_send()

        @pl.when(h == 1)
        def _():
            group(us.at[:, 0:7], u_s).wait_send()

        d_copy.wait_send()
        group(p_v.at[0:7], h_s).wait_send()
        group(er.at[0:14], z_s).wait_send()
        group(gx.at[0, 0:3], n_s).wait_send()
        for j in range(2):
            group(gx.at[j, 0:3, 0:3], f_s.at[j]).wait_send()

    loads[4].wait()
    loads[5].wait()
    swap().wait_recv()
    out = [
        pltpu.make_async_copy(o_v.at[:, 256 * n : 256 * n + 256], out_ref.at[:, 256 * n : 256 * n + 256], st.at[1])
        for n in range(4)
    ]

    def update(there, last):
        block = jnp.concatenate([pr_v[there, 0], pr_v[there, 1]], axis=1)
        high = block.astype(BF16)
        low = (block - high.astype(F32)).astype(BF16)
        both = jnp.concatenate([high, low], axis=0)
        for n in range(4):
            x_high = jnp.concatenate([xh[2 * n + i, there].reshape(256, 128) for i in range(2)], axis=1)
            x_low = jnp.concatenate([xl[2 * n + i, there].reshape(256, 128) for i in range(2)], axis=1)
            one, two = coarse(both, x_high), coarse(high, x_low)
            o_v[:, 256 * n : 256 * n + 256] -= one[:256] + (two + one[256:])
            if last:
                out[n].start()

    update(z, False)

    def step(i):
        p_here(i).wait_recv()
        update(back_z(away(i)), False)

    loop(0, 6, step)
    p_here(6).wait_recv()
    update(back_z(away(6)), True)

    @pl.when(pump)
    def _():
        group(p_v.at[0:14], p_s).wait_send()

    @pl.when(chain)
    def _():
        for j in range(2):
            group(gx.at[j], x_s.at[j]).wait_send()

    adj_out.wait()
    group(o_v, st.at[1]).wait_recv()


def body(diag_inverse, coupling, rhs_top, panel, rhs_rest):
    vmem, sem = pltpu.VMEM, pltpu.SemaphoreType.DMA
    scratch = [
        vmem((2, 64, 64), F32), vmem((64, 64), F32), vmem((2, 64, 1024), F32), vmem((16, 2, 256, 128), F32),
        vmem((8, 2, 256, 128), F32), vmem((256, 1024), F32), vmem((2, 64, 1024), F32), vmem((64, 64), F32),
        vmem((16, 32, 128), F32), vmem((2, 8, 64, 128), F32), vmem((2, 16, 64, 128), F32),
        vmem((16, 64, 128), F32), vmem((16, 64, 128), F32), vmem((8, 64, 128), F32),
        vmem((2, 4, 4, 4, 2, 64, 128), F32), vmem((8, 8, 2, 2, 64, 128), BF16), vmem((8, 8, 2, 2, 64, 128), BF16),
        sem((6,)), sem((2,)), sem, sem((7,)), sem, sem, sem, sem, sem, sem, sem, sem,
        sem, sem((2,)), sem, sem, sem, sem, sem, sem((2, 8)),
        sem, sem((2, 4, 2)), sem((2,)), sem((2,)), sem((2, 4)), sem((2,)), sem((2, 4)),
    ]
    return pl.pallas_call(
        kernel,
        out_shape=(jax.ShapeDtypeStruct((2, 64, 1024), F32), jax.ShapeDtypeStruct((256, 1024), F32)),
        in_specs=[pl.BlockSpec(memory_space=pl.ANY)] * 5,
        out_specs=[pl.BlockSpec(memory_space=pl.ANY)] * 2,
        scratch_shapes=scratch,
        compiler_params=pltpu.CompilerParams(collective_id=0, has_side_effects=True, vmem_limit_bytes=60 * 2**20),
        name="window",
    )(diag_inverse, coupling, rhs_top, panel.reshape(16, 256, 128), rhs_rest)


def solution(mesh):
    in_specs = (
        P(None, "pcol", "prow"),
        P("prow", "pcol"),
        P(None, "prow", None),
        P("prow", "pcol"),
        P(("prow", "pcol"), None),
    )
    out_specs = (P(None, "pcol", None), P(("prow", "pcol"), None))
    return jax.shard_map(body, mesh=mesh, in_specs=in_specs, out_specs=out_specs, check_vma=False)
```

```python
import jax
import jax.numpy as jnp
from jax import lax
from jax.experimental import pallas as pl
from jax.experimental.pallas import tpu as pltpu
from jax.sharding import PartitionSpec as P

MESH = pl.DeviceIdType.MESH
F32, BF16 = jnp.float32, jnp.bfloat16


def precise(a, b):
    return jnp.dot(a, b, precision=lax.Precision.HIGHEST, preferred_element_type=F32)


def coarse(a, b):
    return jnp.dot(a, b, preferred_element_type=F32)


def remote(src, dst, send, recv, device):
    return pltpu.make_async_remote_copy(
        src_ref=src, dst_ref=dst, send_sem=send, recv_sem=recv, device_id=device, device_id_type=MESH
    )


def loop(low, high, body):
    def step(i, carry):
        body(i)
        return carry

    lax.fori_loop(low, high, step, 0)


def kernel(
    d_ref, c_ref, b_ref, p_ref, rest_ref, adj_ref, out_ref,
    d_v, c_v, b_v, p_v, pr_v, o_v, adj_v, d_t,
    cz, us, ur, es, er, eg, gx, xh, xl, tf, th,
    ld, st, p_s, p_r, t_r, h_s, h_r, w_s, w_r, d_s, d_r, c_s, c_r, u_s, u_r, e_s, e_r, g_s, g_r, z_s, z_r, n_s, n_r, o_r, q_r, f_s, f_r, x_s, x_r,
):
    r, c = lax.axis_index("prow"), lax.axis_index("pcol")
    x, y, z, k = r // 4, r % 4, c // 2, c % 2
    h = r % 2
    twin = c + 1 - 2 * k
    pump, chain = k == 0, k == 1

    def row(d):
        return (r + d) % 16

    def at_z(d):
        return (z + d) % 8

    def back_z(d):
        return (z + 8 - d) % 8

    loads = [
        pltpu.make_async_copy(src, dst, ld.at[i])
        for i, (src, dst) in enumerate(
            [(d_ref, d_v), (c_ref, c_v), (b_ref, b_v), (p_ref, p_v.at[:, 0]), (rest_ref, o_v), (p_ref.at[c], pr_v.at[z, k])]
        )
    ]
    for load in loads:
        load.start()

    barrier = pltpu.get_barrier_semaphore()

    def greet(*device):
        pl.semaphore_signal(barrier, inc=1, device_id=device, device_id_type=MESH)

    greet(r, twin)
    loop(2, 16, lambda d: greet(r, (2 * z + d) % 16))

    loop(1, 16, lambda d: greet(row(d), c))

    @pl.when(chain & (h == 0))
    def _():
        loop(1, 16, lambda d: greet(row(d), twin))

    @pl.when(chain & (h == 1))
    def _():
        loop(1, 8, lambda d: greet(row(2 * d), twin))

    for load in loads[:3]:
        load.wait()
    for j in range(2):
        u = precise(d_v[j], b_v[j])
        for n in range(8):
            us[j, n] = u[:, 128 * n : 128 * n + 128]
    cz[c] = jnp.concatenate([c_v[:32], c_v[32:]], axis=1)

    @pl.when(chain & (h == 1))
    def _():
        for j in range(2):
            pltpu.make_async_copy(us.at[j, r // 2], ur.at[j, r], u_r.at[j]).start()

    loads[3].wait()

    @pl.when(pump)
    def _():
        pl.semaphore_wait(barrier, 37 + 8 * h)

    @pl.when(chain)
    def _():
        pl.semaphore_wait(barrier, 30)

    def ahead(s, d):
        return (z + d * (1 + 6 * s)) % 8

    def behind(s, d):
        return (z + d * (7 - 6 * s)) % 8

    def p_near(kk):
        for s in range(2):
            for i in range(2):
                q = 2 * ahead(s, 1) + i
                remote(p_v.at[q, kk], pr_v.at[z, kk], p_s.at[s], p_r.at[s, 1], (r, q)).start()

    def p_far(s, d):
        if d == 4:
            block, held = p_v.at[2 * ahead(s, 4) + s], th.at[s, 0]
        else:
            block, held = p_v.at[pl.ds(2 * ahead(s, d), 2)], tf.at[s, 3 - d]
        remote(block, held, p_s.at[s], t_r.at[s, 4 - d], (r, 2 * ahead(s, 1))).start()

    def p_pass(s, d, n):
        to = 2 * ahead(s, 1)
        if d == 4:
            held, sem = th.at[s, n - 1], t_r.at[s, (0, 3, 5)[n - 1]]
        else:
            held, sem = (tf.at[s, 3 - d], t_r.at[s, 4 - d]) if n == 1 else (tf.at[s, 2], t_r.at[s, 4])
        group(held, sem).wait_recv()
        if n < d - 1:
            on, sem = (th.at[s, n], t_r.at[s, (3, 5)[n - 1]]) if d == 4 else (tf.at[s, 2], t_r.at[s, 4])
            remote(held, on, p_s.at[s], sem, (r, to)).start()
        elif d == 4:
            remote(held, pr_v.at[behind(s, n)], p_s.at[s], p_r.at[s, 4], (r, to + s)).start()
        else:
            for i in range(2):
                remote(held.at[i], pr_v.at[behind(s, n)], p_s.at[s], p_r.at[s, d], (r, to + i)).start()

    def both_ways(body):
        for s in range(2):
            body(s)

    def p_here(i):
        d, s = (i + 1) // 2, (i + 1) % 2
        block = pr_v.at[back_z(side(i))]
        return group(block, p_r.at[s, d])

    def hand(n, i):
        q = 2 * at_z((4 + (2 * (n % 2) - 1) * ((n + 1) // 2)) % 8) + i
        return remote(p_v.at[q, 0], p_v.at[q, 1], h_s, h_r.at[(n + 1) // 4], (r, twin))

    def swap():
        return remote(p_v.at[twin, 0], pr_v.at[z, k], w_s, w_r, (r, twin))

    def group(block, sem):
        return remote(block, block, sem, sem, (r, twin))

    d_copy = remote(d_v.at[1], d_t, d_s, d_r, (r, twin))

    def c_copy(d):
        return remote(cz.at[c], cz.at[c], c_s, c_r, (r, 2 * at_z(d)))

    def u_send(j):
        def body(n):
            @pl.when(pump | (2 * n + 1 != r))
            def _():
                remote(us.at[j, n], ur.at[j, r], u_s, u_r.at[j], (2 * n + k, 2 * z + 1)).start()

        loop(0, 8, body)

    def e_copy(d):
        return remote(es.at[row(d)], er.at[d], e_s, e_r, (row(d), c))

    def g_copy(d):
        return remote(eg.at[r // 2], eg.at[r // 2], g_s, g_r, (row(2 * d), 2 * z + 1))

    def z_copy(j, d):
        block = gx.at[j, x, y, z // 2, z % 2]
        return remote(block, block, z_s, z_r.at[j, d], (r, 2 * at_z(d) + k))

    def z_pass(j, d, on):
        block = gx.at[j, x, y, back_z(d) // 2, back_z(d) % 2]
        return remote(block, block, z_s, z_r.at[j, (d + on) % 8], (r, 2 * at_z(on) + k))

    def z_here(j, d):
        block = gx.at[j, x, y, back_z(d) // 2, back_z(d) % 2]
        return remote(block, block, z_s, z_r.at[j, d], (r, c))

    def along(axis, d):
        return (((x + d) % 4) * 4 + y, c) if axis == 0 else (x * 4 + (y + d) % 4, c)

    def n_copy(j, axis, d, i, a):
        block = gx.at[j, x, y, i, a]
        sem = n_r.at[j, i, a] if axis == a else q_r.at[j, i, a] if d == 2 else o_r.at[j]
        return remote(block, block, n_s, sem, along(axis, d))

    def f_copy(j, i, a, dx, dy, mx, my):
        block = gx.at[j, (x + 4 - dx) % 4, (y + 4 - dy) % 4, i, a]
        across, down = (dx + mx) % 4, (dy + my) % 4
        sem = f_r.at[j, jnp.where(across == 2, 4 + down, across)]
        return remote(block, block, f_s.at[j], sem, (((x + mx) % 4) * 4 + (y + my) % 4, c))

    def x_copy(j, e, d=None):
        block = gx.at[j, (x + 4 - e) % 4] if d is None else gx.at[j, (x + 4 - e) % 4, (y + 4 - d) % 4]
        return remote(block, block, x_s.at[j], x_r.at[j, e if d is None else 4 + d], (r, twin))

    def split(j, e, d):
        xx, yy = (x + 4 - e) % 4, (y + 4 - d) % 4
        p, hh = 2 * xx + yy // 2, yy % 2

        def body(i):
            value = gx[j, xx, yy, i // 2, i % 2]
            high = value.astype(BF16)
            xh[p, i, hh, j] = high
            xl[p, i, hh, j] = (value - high.astype(F32)).astype(BF16)

        loop(0, 8, body)

    def side(i):
        return ((2 * (i % 2) - 1) * ((i + 1) // 2) + 8) % 8

    def z_send(j):
        for d in (2, 6, 1, 7):
            z_copy(j, d).start()

    def turn(i):
        pair = (i + 1) // 2
        return side(i + jnp.where(pair == 1, 2, jnp.where(pair == 2, -2, 0)))

    def spread(j):
        def body(i):
            @pl.when(i > 0)
            def _():
                z_here(j, turn(i)).wait_recv()

            @pl.when(i == 1)
            def _():
                z_pass(j, 2, 1).start()

                @pl.when(back_z(2) % 2 == 0)
                def _():
                    z_pass(j, 2, 2).start()

            @pl.when(i == 2)
            def _():
                z_pass(j, 6, 7).start()

                @pl.when(back_z(6) % 2 == 1)
                def _():
                    z_pass(j, 6, 6).start()

            piece = back_z(turn(i))
            for a in range(2):

                @pl.when(piece % 2 == a)
                def _():
                    for axis in (a, 1 - a):
                        for d in (1, 3, 2):
                            n_copy(j, axis, d, piece // 2, a).start()

        loop(0, 8, body)

    def forward(j):
        def body(i):
            piece = back_z(turn(i))
            n, a = piece // 2, piece % 2
            group(gx.at[j, 0:3, y, n, a], n_r.at[j, n, a]).wait_recv()
            b = 1 - a
            for e, goals in ((1, (1, 3)), (3, (1, 3)), (2, (1, 3, 2))):
                for d in goals:
                    f_copy(j, n, a, b * e, a * e, a * d, b * d).start()
            group(gx.at[j, x, y, n, a], q_r.at[j, n, a]).wait_recv()
            for d in (1, 3):
                f_copy(j, n, a, 2 * a, 2 * b, b * d, a * d).start()

        loop(0, 8, body)
        group(gx.at[j, 0:2, 0], o_r.at[j]).wait_recv()

    def take(j, e):
        loop(0, 4, lambda d: split(j, e, d))

    def cross(j):
        for e in (0, 1, 3):
            if e:
                group(gx.at[j, x, 0:3], f_r.at[j, e]).wait_recv()
            x_copy(j, e).start()
            take(j, e)
        for d in (0, 1, 3, 2):
            if d:
                group(gx.at[j, x, y], f_r.at[j, 4 + d]).wait_recv()
            x_copy(j, 2, d).start()
            split(j, 2, d)

    @pl.when(pump)
    def _():
        loop(1, 8, lambda d: c_copy(d).start())
        u_send(0)
        p_near(0)
        swap().start()
        group(p_v.at[0:3], h_r.at[0]).wait_recv()
        both_ways(lambda s: p_far(s, 4))
        both_ways(lambda s: p_far(s, 3))
        group(p_v.at[0:4], h_r.at[1]).wait_recv()
        both_ways(lambda s: p_far(s, 2))
        p_near(1)

        d_copy.wait_recv()
        group(cz.at[0:15], c_r).wait_recv()
        both = jnp.concatenate([d_v[1], d_t[...]], axis=0)
        for n in range(8):
            upper = jnp.concatenate([cz[2 * n][:, :64], cz[2 * n + 1][:, :64]], axis=1)
            lower = jnp.concatenate([cz[2 * n][:, 64:], cz[2 * n + 1][:, 64:]], axis=1)
            e = precise(both, jnp.concatenate([upper, lower], axis=0))
            es[2 * n] = e[:64]
            es[2 * n + 1] = e[64:]
        loop(1, 16, lambda d: e_copy(d).start())
        u_send(1)

        both_ways(lambda s: p_pass(s, 4, 1))

        group(er.at[1:16], e_r).wait_recv()
        er[0] = es[r]
        eg[r // 2] = sum(er[d] for d in range(16))
        loop(0, 8, lambda d: g_copy(d).start())
        both_ways(lambda s: p_pass(s, 3, 1))
        both_ways(lambda s: p_pass(s, 2, 1))
        both_ways(lambda s: p_pass(s, 4, 2))
        both_ways(lambda s: p_pass(s, 3, 2))
        both_ways(lambda s: p_pass(s, 4, 3))

        for j in range(2):
            for e in (0, 1, 3):
                x_copy(j, e).wait_recv()
                take(j, e)
            for d in (0, 1, 3, 2):
                x_copy(j, 2, d).wait_recv()
                split(j, 2, d)

    @pl.when(chain)
    def _():
        u_send(0)
        loop(0, 8, lambda d: c_copy(d).start())
        d_copy.start()
        swap().start()
        loop(0, 14, lambda i: hand(i // 2, i % 2).start())

        group(ur.at[0], u_r.at[0]).wait_recv()
        gx[0, x, y, z // 2, z % 2] = sum(ur[0, i] for i in range(16))
        z_send(0)
        u_send(1)
        spread(0)
        forward(0)

        group(ur.at[1], u_r.at[1]).wait_recv()
        total = sum(ur[1, i] for i in range(16))
        tile = [gx[0, x, 2 * (y // 2) + hh, n // 2, n % 2] for n in range(8) for hh in range(2)]
        group(eg, g_r).wait_recv()
        e = jnp.concatenate([eg[n] for n in range(8)], axis=1)
        gx[1, x, y, z // 2, z % 2] = total - precise(e, jnp.concatenate(tile, axis=0))
        z_send(1)
        spread(1)
        cross(0)
        forward(1)
        cross(1)

    for n in range(8):
        for j in range(2):
            adj_v[j, :, 128 * n : 128 * n + 128] = gx[j, n // 2, 2 * (n % 2) + k, z // 2, z % 2]
    adj_out = pltpu.make_async_copy(adj_v, adj_ref, st.at[0])
    adj_out.start()

    swap().wait_send()

    @pl.when(pump)
    def _():
        group(cz.at[0:7], c_s).wait_send()
        group(us, u_s).wait_send()
        group(es.at[0:15], e_s).wait_send()
        group(eg, g_s).wait_send()

    @pl.when(chain)
    def _():
        group(cz.at[0:8], c_s).wait_send()

        @pl.when(h == 0)
        def _():
            group(us, u_s).wait_send()

        @pl.when(h == 1)
        def _():
            group(us.at[:, 0:7], u_s).wait_send()

        d_copy.wait_send()
        group(p_v.at[0:7], h_s).wait_send()
        group(er.at[0:14], z_s).wait_send()
        group(gx.at[0, 0:3], n_s).wait_send()
        for j in range(2):
            group(gx.at[j, 0:3, 0:3], f_s.at[j]).wait_send()

    loads[4].wait()
    loads[5].wait()
    swap().wait_recv()
    out = [
        pltpu.make_async_copy(o_v.at[:, 256 * n : 256 * n + 256], out_ref.at[:, 256 * n : 256 * n + 256], st.at[1])
        for n in range(4)
    ]

    def update(there, last):
        block = jnp.concatenate([pr_v[there, 0], pr_v[there, 1]], axis=1)
        high = block.astype(BF16)
        low = (block - high.astype(F32)).astype(BF16)
        both = jnp.concatenate([high, low], axis=0)
        for n in range(4):
            x_high = jnp.concatenate([xh[2 * n + i, there].reshape(256, 128) for i in range(2)], axis=1)
            x_low = jnp.concatenate([xl[2 * n + i, there].reshape(256, 128) for i in range(2)], axis=1)
            one, two = coarse(both, x_high), coarse(high, x_low)
            o_v[:, 256 * n : 256 * n + 256] -= one[:256] + (two + one[256:])
            if last:
                out[n].start()

    update(z, False)

    def step(i):
        p_here(i).wait_recv()
        update(back_z(side(i)), False)

    loop(1, 7, step)
    group(pr_v.at[back_z(4)], p_r.at[k, 4]).wait_recv()
    update(back_z(4), True)

    @pl.when(pump)
    def _():
        for s in range(2):
            group(gx.at[0], p_s.at[s]).wait_send()

    @pl.when(chain)
    def _():
        for j in range(2):
            group(gx.at[j], x_s.at[j]).wait_send()

    adj_out.wait()
    group(o_v, st.at[1]).wait_recv()


def body(diag_inverse, coupling, rhs_top, panel, rhs_rest):
    vmem, sem = pltpu.VMEM, pltpu.SemaphoreType.DMA
    scratch = [
        vmem((2, 64, 64), F32), vmem((64, 64), F32), vmem((2, 64, 1024), F32), vmem((16, 2, 256, 128), F32),
        vmem((8, 2, 256, 128), F32), vmem((256, 1024), F32), vmem((2, 64, 1024), F32), vmem((64, 64), F32),
        vmem((16, 32, 128), F32), vmem((2, 8, 64, 128), F32), vmem((2, 16, 64, 128), F32),
        vmem((16, 64, 128), F32), vmem((16, 64, 128), F32), vmem((8, 64, 128), F32),
        vmem((2, 4, 4, 4, 2, 64, 128), F32), vmem((8, 8, 2, 2, 64, 128), BF16), vmem((8, 8, 2, 2, 64, 128), BF16),
        vmem((2, 3, 2, 2, 256, 128), F32), vmem((2, 3, 2, 256, 128), F32),
        sem((6,)), sem((2,)), sem((2,)), sem((2, 5)), sem((2, 6)), sem, sem((2,)), sem, sem, sem, sem, sem, sem,
        sem, sem((2,)), sem, sem, sem, sem, sem, sem((2, 8)),
        sem, sem((2, 4, 2)), sem((2,)), sem((2, 4, 2)), sem((2,)), sem((2, 8)), sem((2,)), sem((2, 8)),
    ]
    return pl.pallas_call(
        kernel,
        out_shape=(jax.ShapeDtypeStruct((2, 64, 1024), F32), jax.ShapeDtypeStruct((256, 1024), F32)),
        in_specs=[pl.BlockSpec(memory_space=pl.ANY)] * 5,
        out_specs=[pl.BlockSpec(memory_space=pl.ANY)] * 2,
        scratch_shapes=scratch,
        compiler_params=pltpu.CompilerParams(collective_id=0, has_side_effects=True, vmem_limit_bytes=60 * 2**20),
        name="window",
    )(diag_inverse, coupling, rhs_top, panel.reshape(16, 256, 128), rhs_rest)


def solution(mesh):
    in_specs = (
        P(None, "pcol", "prow"),
        P("prow", "pcol"),
        P(None, "prow", None),
        P("prow", "pcol"),
        P(("prow", "pcol"), None),
    )
    out_specs = (P(None, "pcol", None), P(("prow", "pcol"), None))
    return jax.shard_map(body, mesh=mesh, in_specs=in_specs, out_specs=out_specs, check_vma=False)
```

```python
import jax
import jax.numpy as jnp
from jax import lax
from jax.experimental import pallas as pl
from jax.experimental.pallas import tpu as pltpu
from jax.sharding import PartitionSpec as P

MESH = pl.DeviceIdType.MESH
F32, BF16 = jnp.float32, jnp.bfloat16


def precise(a, b):
    return jnp.dot(a, b, precision=lax.Precision.HIGHEST, preferred_element_type=F32)


def coarse(a, b):
    return jnp.dot(a, b, preferred_element_type=F32)


def remote(src, dst, send, recv, device):
    return pltpu.make_async_remote_copy(
        src_ref=src, dst_ref=dst, send_sem=send, recv_sem=recv, device_id=device, device_id_type=MESH
    )


def loop(low, high, body):
    def step(i, carry):
        body(i)
        return carry

    lax.fori_loop(low, high, step, 0)


def kernel(
    d_ref, c_ref, b_ref, p_ref, rest_ref, adj_ref, out_ref,
    d_v, c_v, b_v, p_v, pr_v, o_v, adj_v, d_t,
    cz, us, ur, es, er, eg, gx, xh, xl, tf, th,
    ld, st, p_s, p_r, t_r, h_s, h_r, w_s, w_r, d_s, d_r, c_s, c_r, u_s, u_r, e_s, e_r, g_s, g_r, z_s, z_r, n_s, n_r, o_r, q_r, f_s, f_r, x_s, x_r,
):
    r, c = lax.axis_index("prow"), lax.axis_index("pcol")
    x, y, z, k = r // 4, r % 4, c // 2, c % 2
    h = r % 2
    twin = c + 1 - 2 * k
    pump, chain = k == 0, k == 1

    def row(d):
        return (r + d) % 16

    def at_z(d):
        return (z + d) % 8

    def back_z(d):
        return (z + 8 - d) % 8

    loads = [
        pltpu.make_async_copy(src, dst, ld.at[i])
        for i, (src, dst) in enumerate(
            [(d_ref, d_v), (c_ref, c_v), (b_ref, b_v), (p_ref, p_v.at[:, 0]), (rest_ref, o_v), (p_ref.at[c], pr_v.at[z, k])]
        )
    ]
    for load in loads:
        load.start()

    barrier = pltpu.get_barrier_semaphore()

    def greet(*device):
        pl.semaphore_signal(barrier, inc=1, device_id=device, device_id_type=MESH)

    greet(r, twin)
    loop(2, 16, lambda d: greet(r, (2 * z + d) % 16))

    loop(1, 16, lambda d: greet(row(d), c))

    @pl.when(chain & (h == 0))
    def _():
        loop(1, 16, lambda d: greet(row(d), twin))

    @pl.when(chain & (h == 1))
    def _():
        loop(1, 8, lambda d: greet(row(2 * d), twin))

    for load in loads[:3]:
        load.wait()
    for j in range(2):
        u = precise(d_v[j], b_v[j])
        for n in range(8):
            us[j, n] = u[:, 128 * n : 128 * n + 128]
    cz[c] = jnp.concatenate([c_v[:32], c_v[32:]], axis=1)

    @pl.when(chain & (h == 1))
    def _():
        for j in range(2):
            pltpu.make_async_copy(us.at[j, r // 2], ur.at[j, r], u_r.at[j]).start()

    loads[3].wait()

    @pl.when(pump)
    def _():
        pl.semaphore_wait(barrier, 37 + 8 * h)

    @pl.when(chain)
    def _():
        pl.semaphore_wait(barrier, 30)

    def ahead(s, d):
        return (z + d * (1 + 6 * s)) % 8

    def behind(s, d):
        return (z + d * (7 - 6 * s)) % 8

    def p_near(kk):
        for s in range(2):
            for i in range(2):
                q = 2 * ahead(s, 1) + i
                remote(p_v.at[q, kk], pr_v.at[z, kk], p_s.at[s], p_r.at[s, 1], (r, q)).start()

    def p_far(s, d):
        if d == 4:
            block, held = p_v.at[2 * ahead(s, 4) + s], th.at[s, 0]
        else:
            block, held = p_v.at[pl.ds(2 * ahead(s, d), 2)], tf.at[s, 3 - d]
        remote(block, held, p_s.at[s], t_r.at[s, 4 - d], (r, 2 * ahead(s, 1))).start()

    def p_pass(s, d, n):
        to = 2 * ahead(s, 1)
        if d == 4:
            held, sem = th.at[s, n - 1], t_r.at[s, (0, 3, 5)[n - 1]]
        else:
            held, sem = (tf.at[s, 3 - d], t_r.at[s, 4 - d]) if n == 1 else (tf.at[s, 2], t_r.at[s, 4])
        group(held, sem).wait_recv()
        if n < d - 1:
            on, sem = (th.at[s, n], t_r.at[s, (3, 5)[n - 1]]) if d == 4 else (tf.at[s, 2], t_r.at[s, 4])
            remote(held, on, p_s.at[s], sem, (r, to)).start()
        elif d == 4:
            remote(held, pr_v.at[behind(s, n)], p_s.at[s], p_r.at[s, 4], (r, to + s)).start()
        else:
            for i in range(2):
                remote(held.at[i], pr_v.at[behind(s, n)], p_s.at[s], p_r.at[s, d], (r, to + i)).start()

    def both_ways(body):
        for s in range(2):
            body(s)

    def p_here(i):
        d, s = (i + 1) // 2, (i + 1) % 2
        block = pr_v.at[back_z(side(i))]
        return group(block, p_r.at[s, d])

    def hand(n, i):
        q = 2 * at_z((4 + (2 * (n % 2) - 1) * ((n + 1) // 2)) % 8) + i
        return remote(p_v.at[q, 0], p_v.at[q, 1], h_s, h_r.at[(n + 1) // 4], (r, twin))

    def swap():
        return remote(p_v.at[twin, 0], pr_v.at[z, k], w_s, w_r, (r, twin))

    def group(block, sem):
        return remote(block, block, sem, sem, (r, twin))

    d_copy = remote(d_v.at[1], d_t, d_s, d_r, (r, twin))

    def c_copy(d):
        return remote(cz.at[c], cz.at[c], c_s, c_r, (r, 2 * at_z(d)))

    def u_send(j):
        def body(n):
            @pl.when(pump | (2 * n + 1 != r))
            def _():
                remote(us.at[j, n], ur.at[j, r], u_s, u_r.at[j], (2 * n + k, 2 * z + 1)).start()

        loop(0, 8, body)

    def e_copy(d):
        return remote(es.at[row(d)], er.at[d], e_s, e_r, (row(d), c))

    def g_copy(d):
        return remote(eg.at[r // 2], eg.at[r // 2], g_s, g_r, (row(2 * d), 2 * z + 1))

    def z_copy(j, d):
        block = gx.at[j, x, y, z // 2, z % 2]
        return remote(block, block, z_s, z_r.at[j, d], (r, 2 * at_z(d) + k))

    def z_pass(j, d, on):
        block = gx.at[j, x, y, back_z(d) // 2, back_z(d) % 2]
        return remote(block, block, z_s, z_r.at[j, (d + on) % 8], (r, 2 * at_z(on) + k))

    def z_here(j, d):
        block = gx.at[j, x, y, back_z(d) // 2, back_z(d) % 2]
        return remote(block, block, z_s, z_r.at[j, d], (r, c))

    def along(axis, d):
        return (((x + d) % 4) * 4 + y, c) if axis == 0 else (x * 4 + (y + d) % 4, c)

    def n_copy(j, axis, d, i, a):
        block = gx.at[j, x, y, i, a]
        sem = n_r.at[j, i, a] if axis == a else q_r.at[j, i, a] if d == 2 else o_r.at[j]
        return remote(block, block, n_s, sem, along(axis, d))

    def f_copy(j, i, a, dx, dy, mx, my):
        block = gx.at[j, (x + 4 - dx) % 4, (y + 4 - dy) % 4, i, a]
        across, down = (dx + mx) % 4, (dy + my) % 4
        sem = f_r.at[j, jnp.where(across == 2, 4 + down, across)]
        return remote(block, block, f_s.at[j], sem, (((x + mx) % 4) * 4 + (y + my) % 4, c))

    def x_copy(j, e, d=None):
        block = gx.at[j, (x + 4 - e) % 4] if d is None else gx.at[j, (x + 4 - e) % 4, (y + 4 - d) % 4]
        return remote(block, block, x_s.at[j], x_r.at[j, e if d is None else 4 + d], (r, twin))

    def split(j, e, d):
        xx, yy = (x + 4 - e) % 4, (y + 4 - d) % 4
        p, hh = 2 * xx + yy // 2, yy % 2

        def body(i):
            value = gx[j, xx, yy, i // 2, i % 2]
            high = value.astype(BF16)
            xh[p, i, hh, j] = high
            xl[p, i, hh, j] = (value - high.astype(F32)).astype(BF16)

        loop(0, 8, body)

    def side(i):
        return ((2 * (i % 2) - 1) * ((i + 1) // 2) + 8) % 8

    def z_send(j):
        for d in (2, 6, 1, 7):
            z_copy(j, d).start()

    def turn(i):
        pair = (i + 1) // 2
        return side(i + jnp.where(pair == 1, 2, jnp.where(pair == 2, -2, 0)))

    def spread(j):
        def body(i):
            @pl.when(i > 0)
            def _():
                z_here(j, turn(i)).wait_recv()

            @pl.when(i == 1)
            def _():
                z_pass(j, 2, 1).start()

                @pl.when(back_z(2) % 2 == 0)
                def _():
                    z_pass(j, 2, 2).start()

            @pl.when(i == 2)
            def _():
                z_pass(j, 6, 7).start()

                @pl.when(back_z(6) % 2 == 1)
                def _():
                    z_pass(j, 6, 6).start()

            piece = back_z(turn(i))
            for a in range(2):

                @pl.when(piece % 2 == a)
                def _():
                    for axis in (a, 1 - a):
                        for d in (1, 3, 2):
                            n_copy(j, axis, d, piece // 2, a).start()

        loop(0, 8, body)

    def forward(j):
        def body(i):
            piece = back_z(turn(i))
            n, a = piece // 2, piece % 2
            group(gx.at[j, 0:3, y, n, a], n_r.at[j, n, a]).wait_recv()
            b = 1 - a
            for e, goals in ((1, (1, 3)), (3, (1, 3)), (2, (1, 3, 2))):
                for d in goals:
                    f_copy(j, n, a, b * e, a * e, a * d, b * d).start()
            group(gx.at[j, x, y, n, a], q_r.at[j, n, a]).wait_recv()
            for d in (1, 3):
                f_copy(j, n, a, 2 * a, 2 * b, b * d, a * d).start()

        loop(0, 8, body)
        group(gx.at[j, 0:2, 0], o_r.at[j]).wait_recv()

    def take(j, e):
        loop(0, 4, lambda d: split(j, e, d))

    def cross(j):
        for e in (0, 1, 3):
            if e:
                group(gx.at[j, x, 0:3], f_r.at[j, e]).wait_recv()
            x_copy(j, e).start()
            take(j, e)
        for d in (0, 1, 3, 2):
            if d:
                group(gx.at[j, x, y], f_r.at[j, 4 + d]).wait_recv()
            x_copy(j, 2, d).start()
            split(j, 2, d)

    @pl.when(pump)
    def _():
        loop(1, 8, lambda d: c_copy(d).start())
        u_send(0)
        p_near(0)
        swap().start()
        group(p_v.at[0:3], h_r.at[0]).wait_recv()
        both_ways(lambda s: p_far(s, 4))
        both_ways(lambda s: p_far(s, 3))
        group(p_v.at[0:4], h_r.at[1]).wait_recv()
        both_ways(lambda s: p_far(s, 2))
        p_near(1)

        d_copy.wait_recv()
        group(cz.at[0:15], c_r).wait_recv()
        both = jnp.concatenate([d_v[1], d_t[...]], axis=0)
        for n in range(8):
            upper = jnp.concatenate([cz[2 * n][:, :64], cz[2 * n + 1][:, :64]], axis=1)
            lower = jnp.concatenate([cz[2 * n][:, 64:], cz[2 * n + 1][:, 64:]], axis=1)
            e = precise(both, jnp.concatenate([upper, lower], axis=0))
            es[2 * n] = e[:64]
            es[2 * n + 1] = e[64:]
        loop(1, 16, lambda d: e_copy(d).start())
        u_send(1)

        both_ways(lambda s: p_pass(s, 4, 1))

        group(er.at[1:16], e_r).wait_recv()
        er[0] = es[r]
        eg[r // 2] = sum(er[d] for d in range(16))
        loop(0, 8, lambda d: g_copy(d).start())
        both_ways(lambda s: p_pass(s, 3, 1))
        both_ways(lambda s: p_pass(s, 2, 1))
        both_ways(lambda s: p_pass(s, 4, 2))
        both_ways(lambda s: p_pass(s, 3, 2))
        both_ways(lambda s: p_pass(s, 4, 3))

        for j in range(2):
            for e in (0, 1, 3):
                x_copy(j, e).wait_recv()
                take(j, e)
            for d in (0, 1, 3, 2):
                x_copy(j, 2, d).wait_recv()
                split(j, 2, d)

    @pl.when(chain)
    def _():
        u_send(0)
        loop(0, 8, lambda d: c_copy(d).start())
        d_copy.start()
        swap().start()
        loop(0, 14, lambda i: hand(i // 2, i % 2).start())

        group(ur.at[0], u_r.at[0]).wait_recv()
        gx[0, x, y, z // 2, z % 2] = sum(ur[0, i] for i in range(16))
        z_send(0)
        u_send(1)
        spread(0)
        forward(0)

        group(ur.at[1], u_r.at[1]).wait_recv()
        total = sum(ur[1, i] for i in range(16))
        tile = [gx[0, x, 2 * (y // 2) + hh, n // 2, n % 2] for n in range(8) for hh in range(2)]
        group(eg, g_r).wait_recv()
        e = jnp.concatenate([eg[n] for n in range(8)], axis=1)
        gx[1, x, y, z // 2, z % 2] = total - precise(e, jnp.concatenate(tile, axis=0))
        z_send(1)
        spread(1)
        cross(0)
        forward(1)
        cross(1)

    for n in range(8):
        for j in range(2):
            adj_v[j, :, 128 * n : 128 * n + 128] = gx[j, n // 2, 2 * (n % 2) + k, z // 2, z % 2]
    adj_out = pltpu.make_async_copy(adj_v, adj_ref, st.at[0])
    adj_out.start()

    swap().wait_send()

    @pl.when(pump)
    def _():
        group(cz.at[0:7], c_s).wait_send()
        group(us, u_s).wait_send()
        group(es.at[0:15], e_s).wait_send()
        group(eg, g_s).wait_send()

    @pl.when(chain)
    def _():
        group(cz.at[0:8], c_s).wait_send()

        @pl.when(h == 0)
        def _():
            group(us, u_s).wait_send()

        @pl.when(h == 1)
        def _():
            group(us.at[:, 0:7], u_s).wait_send()

        d_copy.wait_send()
        group(p_v.at[0:7], h_s).wait_send()
        group(er.at[0:14], z_s).wait_send()
        group(gx.at[0, 0:3], n_s).wait_send()
        for j in range(2):
            group(gx.at[j, 0:3, 0:3], f_s.at[j]).wait_send()

    loads[4].wait()
    loads[5].wait()
    swap().wait_recv()
    out = [
        pltpu.make_async_copy(o_v.at[:, 256 * n : 256 * n + 256], out_ref.at[:, 256 * n : 256 * n + 256], st.at[1])
        for n in range(4)
    ]

    def update(there, last):
        block = jnp.concatenate([pr_v[there, 0], pr_v[there, 1]], axis=1)
        high = block.astype(BF16)
        low = (block - high.astype(F32)).astype(BF16)
        both = jnp.concatenate([high, low], axis=0)
        for n in range(4):
            x_high = jnp.concatenate([xh[2 * n + i, there].reshape(256, 128) for i in range(2)], axis=1)
            x_low = jnp.concatenate([xl[2 * n + i, there].reshape(256, 128) for i in range(2)], axis=1)
            one, two = coarse(both, x_high), coarse(high, x_low)
            o_v[:, 256 * n : 256 * n + 256] -= one[:256] + (two + one[256:])
            if last:
                out[n].start()

    update(z, False)

    def step(i):
        p_here(i).wait_recv()
        update(back_z(side(i)), False)

    loop(1, 7, step)
    group(pr_v.at[back_z(4)], p_r.at[k, 4]).wait_recv()
    update(back_z(4), True)

    @pl.when(pump)
    def _():
        for s in range(2):
            group(gx.at[0], p_s.at[s]).wait_send()

    @pl.when(chain)
    def _():
        for j in range(2):
            group(gx.at[j], x_s.at[j]).wait_send()

    adj_out.wait()
    group(o_v, st.at[1]).wait_recv()


def settle(adj_ref, out_ref, adj_to, out_to, adj_v, out_v, in_s, to_s):
    parts = [(out_ref, out_v, out_to, pl.ds(64 * i, 64), 0) for i in range(4)]
    parts += [(adj_ref, adj_v, adj_to, pl.ds(i, 1), 1) for i in range(2)]
    loads = [pltpu.make_async_copy(src.at[at], held.at[at], in_s.at[i]) for i, (src, held, _, at, _) in enumerate(parts)]
    for load in loads:
        load.start()
    for load, (_, held, to, at, n) in zip(loads, parts):
        load.wait()
        pltpu.make_async_copy(held.at[at], to.at[at], to_s.at[n]).start()
    pltpu.make_async_copy(out_v, out_to, to_s.at[0]).wait()
    pltpu.make_async_copy(adj_v, adj_to, to_s.at[1]).wait()


def body(diag_inverse, coupling, rhs_top, panel, rhs_rest):
    vmem, sem = pltpu.VMEM, pltpu.SemaphoreType.DMA
    scratch = [
        vmem((2, 64, 64), F32), vmem((64, 64), F32), vmem((2, 64, 1024), F32), vmem((16, 2, 256, 128), F32),
        vmem((8, 2, 256, 128), F32), vmem((256, 1024), F32), vmem((2, 64, 1024), F32), vmem((64, 64), F32),
        vmem((16, 32, 128), F32), vmem((2, 8, 64, 128), F32), vmem((2, 16, 64, 128), F32),
        vmem((16, 64, 128), F32), vmem((16, 64, 128), F32), vmem((8, 64, 128), F32),
        vmem((2, 4, 4, 4, 2, 64, 128), F32), vmem((8, 8, 2, 2, 64, 128), BF16), vmem((8, 8, 2, 2, 64, 128), BF16),
        vmem((2, 3, 2, 2, 256, 128), F32), vmem((2, 3, 2, 256, 128), F32),
        sem((6,)), sem((2,)), sem((2,)), sem((2, 5)), sem((2, 6)), sem, sem((2,)), sem, sem, sem, sem, sem, sem,
        sem, sem((2,)), sem, sem, sem, sem, sem, sem((2, 8)),
        sem, sem((2, 4, 2)), sem((2,)), sem((2, 4, 2)), sem((2,)), sem((2, 8)), sem((2,)), sem((2, 8)),
    ]
    shapes = (jax.ShapeDtypeStruct((2, 64, 1024), F32), jax.ShapeDtypeStruct((256, 1024), F32))
    results = pl.pallas_call(
        kernel,
        out_shape=shapes,
        in_specs=[pl.BlockSpec(memory_space=pl.ANY)] * 5,
        out_specs=[pl.BlockSpec(memory_space=pl.ANY)] * 2,
        scratch_shapes=scratch,
        compiler_params=pltpu.CompilerParams(collective_id=0, has_side_effects=True, vmem_limit_bytes=60 * 2**20),
        name="window",
    )(diag_inverse, coupling, rhs_top, panel.reshape(16, 256, 128), rhs_rest)
    return pl.pallas_call(
        settle,
        out_shape=shapes,
        in_specs=[pl.BlockSpec(memory_space=pl.ANY)] * 2,
        out_specs=[pl.BlockSpec(memory_space=pl.ANY)] * 2,
        scratch_shapes=[vmem((2, 64, 1024), F32), vmem((256, 1024), F32), sem((6,)), sem((2,))],
        compiler_params=pltpu.CompilerParams(vmem_limit_bytes=60 * 2**20),
        name="settle",
    )(*results)


def solution(mesh):
    in_specs = (
        P(None, "pcol", "prow"),
        P("prow", "pcol"),
        P(None, "prow", None),
        P("prow", "pcol"),
        P(("prow", "pcol"), None),
    )
    out_specs = (P(None, "pcol", None), P(("prow", "pcol"), None))
    return jax.shard_map(body, mesh=mesh, in_specs=in_specs, out_specs=out_specs, check_vma=False)
```

```python
import jax
import jax.numpy as jnp
from jax import lax
from jax.experimental import pallas as pl
from jax.experimental.pallas import tpu as pltpu
from jax.sharding import PartitionSpec as P

MESH = pl.DeviceIdType.MESH
F32, BF16 = jnp.float32, jnp.bfloat16


def precise(a, b):
    return jnp.dot(a, b, precision=lax.Precision.HIGHEST, preferred_element_type=F32)


def coarse(a, b):
    return jnp.dot(a, b, preferred_element_type=F32)


def remote(src, dst, send, recv, device):
    return pltpu.make_async_remote_copy(
        src_ref=src, dst_ref=dst, send_sem=send, recv_sem=recv, device_id=device, device_id_type=MESH
    )


def loop(low, high, body):
    def step(i, carry):
        body(i)
        return carry

    lax.fori_loop(low, high, step, 0)


def kernel(
    d_ref, c_ref, b_ref, p_ref, rest_ref, adj_ref, out_ref,
    d_v, c_v, b_v, p_v, pr_v, o_v, adj_v, d_t,
    cz, us, ur, es, er, eg, gx, xh, xl, tf, th,
    ld, st, p_s, p_r, t_r, h_s, h_r, w_s, w_r, d_s, d_r, c_s, c_r, u_s, u_r, e_s, e_r, g_s, g_r, z_s, z_r, n_s, n_r, o_r, f_s, f_r, x_s, x_r,
):
    r, c = lax.axis_index("prow"), lax.axis_index("pcol")
    x, y, z, k = r // 4, r % 4, c // 2, c % 2
    h = r % 2
    twin = c + 1 - 2 * k
    pump, chain = k == 0, k == 1

    def row(d):
        return (r + d) % 16

    def at_z(d):
        return (z + d) % 8

    def back_z(d):
        return (z + 8 - d) % 8

    loads = [
        pltpu.make_async_copy(src, dst, ld.at[i])
        for i, (src, dst) in enumerate(
            [(d_ref, d_v), (c_ref, c_v), (b_ref, b_v), (p_ref, p_v.at[:, 0]), (rest_ref, o_v), (p_ref.at[c], pr_v.at[z, k])]
        )
    ]
    for load in loads:
        load.start()

    barrier = pltpu.get_barrier_semaphore()

    def greet(*device):
        pl.semaphore_signal(barrier, inc=1, device_id=device, device_id_type=MESH)

    greet(r, twin)
    loop(2, 16, lambda d: greet(r, (2 * z + d) % 16))

    loop(1, 16, lambda d: greet(row(d), c))

    @pl.when(chain & (h == 0))
    def _():
        loop(1, 16, lambda d: greet(row(d), twin))

    @pl.when(chain & (h == 1))
    def _():
        loop(1, 8, lambda d: greet(row(2 * d), twin))

    def partial():
        loads[2].wait()
        for j in range(2):
            u = precise(d_v[j], b_v[j])
            for n in range(8):
                us[j, n] = u[:, 128 * n : 128 * n + 128]

    for load in loads[:2]:
        load.wait()
    cz[c] = jnp.concatenate([c_v[:32], c_v[32:]], axis=1)

    @pl.when(chain)
    def _():
        partial()

    @pl.when(chain & (h == 1))
    def _():
        for j in range(2):
            pltpu.make_async_copy(us.at[j, r // 2], ur.at[j, r], u_r.at[j]).start()

    @pl.when(pump)
    def _():
        pl.semaphore_wait(barrier, 37 + 8 * h)

    @pl.when(chain)
    def _():
        pl.semaphore_wait(barrier, 30)

    def ahead(s, d):
        return (z + d * (1 + 6 * s)) % 8

    def behind(s, d):
        return (z + d * (7 - 6 * s)) % 8

    def p_near(kk):
        for s in range(2):
            for i in range(2):
                q = 2 * ahead(s, 1) + i
                block = p_v.at[q, 1] if kk else p_ref.at[q]
                remote(block, pr_v.at[z, kk], p_s.at[s], p_r.at[s, 1], (r, q)).start()

    def p_far(s, d, kk):
        goal = 2 * ahead(s, 4) + s if d == 4 else pl.ds(2 * ahead(s, d), 2)
        block = p_v.at[goal, 1] if kk else p_ref.at[goal]
        held = th.at[s, 0, kk] if d == 4 else tf.at[s, 3 - d, :, kk]
        remote(block, held, p_s.at[s], t_r.at[s, 4 - d], (r, 2 * ahead(s, 1))).start()

    def p_pass(s, d, n):
        to = 2 * ahead(s, 1)
        if d == 4:
            held, sem = th.at[s, n - 1], t_r.at[s, (0, 3, 5)[n - 1]]
        else:
            held, sem = (tf.at[s, 3 - d], t_r.at[s, 4 - d]) if n == 1 else (tf.at[s, 2], t_r.at[s, 4])
        group(held, sem).wait_recv()
        if n < d - 1:
            on, sem = (th.at[s, n], t_r.at[s, (3, 5)[n - 1]]) if d == 4 else (tf.at[s, 2], t_r.at[s, 4])
            remote(held, on, p_s.at[s], sem, (r, to)).start()
        elif d == 4:
            remote(held, pr_v.at[behind(s, n)], p_s.at[s], p_r.at[s, 4], (r, to + s)).start()
        else:
            for i in range(2):
                remote(held.at[i], pr_v.at[behind(s, n)], p_s.at[s], p_r.at[s, d], (r, to + i)).start()

    def both_ways(body):
        for s in range(2):
            body(s)

    def p_here(i):
        d, s = (i + 1) // 2, (i + 1) % 2
        block = pr_v.at[back_z(side(i))]
        return group(block, p_r.at[s, d])

    def hand(n, i):
        q = 2 * at_z((4 + (2 * (n % 2) - 1) * ((n + 1) // 2)) % 8) + i
        return remote(p_v.at[q, 0], p_v.at[q, 1], h_s, h_r.at[(n + 1) // 4], (r, twin))

    def swap():
        return remote(p_v.at[twin, 0], pr_v.at[z, k], w_s, w_r, (r, twin))

    def group(block, sem):
        return remote(block, block, sem, sem, (r, twin))

    d_copy = remote(d_v.at[1], d_t, d_s, d_r, (r, twin))

    def c_copy(d):
        return remote(cz.at[c], cz.at[c], c_s, c_r, (r, 2 * at_z(d)))

    def u_send(j):
        def body(n):
            @pl.when(pump | (2 * n + 1 != r))
            def _():
                remote(us.at[j, n], ur.at[j, r], u_s, u_r.at[j], (2 * n + k, 2 * z + 1)).start()

        loop(0, 8, body)

    def e_copy(d):
        return remote(es.at[row(d)], er.at[d], e_s, e_r, (row(d), c))

    def g_copy(d):
        return remote(eg.at[r // 2], eg.at[r // 2], g_s, g_r, (row(2 * d), 2 * z + 1))

    def z_copy(j, d):
        block = gx.at[j, x, y, z // 2, z % 2]
        return remote(block, block, z_s, z_r.at[j, d], (r, 2 * at_z(d) + k))

    def z_pass(j, d, on):
        block = gx.at[j, x, y, back_z(d) // 2, back_z(d) % 2]
        return remote(block, block, z_s, z_r.at[j, (d + on) % 8], (r, 2 * at_z(on) + k))

    def z_here(j, d):
        block = gx.at[j, x, y, back_z(d) // 2, back_z(d) % 2]
        return remote(block, block, z_s, z_r.at[j, d], (r, c))

    def along(axis, d):
        return (((x + d) % 4) * 4 + y, c) if axis == 0 else (x * 4 + (y + d) % 4, c)

    def n_copy(j, axis, d, i, a):
        block = gx.at[j, x, y, i, a]
        sem = n_r.at[j, i, a] if axis == a or d == 2 else o_r.at[j]
        return remote(block, block, n_s, sem, along(axis, d))

    def f_copy(j, i, a, dx, dy, mx, my):
        block = gx.at[j, (x + 4 - dx) % 4, (y + 4 - dy) % 4, i, a]
        across, down = (dx + mx) % 4, (dy + my) % 4
        sem = f_r.at[j, jnp.where(across == 2, 1 + down, (across - 1) // 2)]
        return remote(block, block, f_s.at[j], sem, (((x + mx) % 4) * 4 + (y + my) % 4, c))

    def x_copy(j, e, d=None):
        block = gx.at[j, (x + 4 - e) % 4] if d is None else gx.at[j, (x + 4 - e) % 4, (y + 4 - d) % 4]
        return remote(block, block, x_s.at[j], x_r.at[j, (e + 1) // 2 if d is None else 3 + d], (r, twin))

    def split(j, e, d):
        xx, yy = (x + 4 - e) % 4, (y + 4 - d) % 4
        p, hh = 2 * xx + yy // 2, yy % 2

        def body(i):
            value = gx[j, xx, yy, i // 2, i % 2]
            high = value.astype(BF16)
            xh[p, i, hh, j] = high
            xl[p, i, hh, j] = (value - high.astype(F32)).astype(BF16)

        loop(0, 8, body)

    def side(i):
        return ((2 * (i % 2) - 1) * ((i + 1) // 2) + 8) % 8

    def z_send(j):
        for d in (2, 6, 1, 7):
            z_copy(j, d).start()

    def turn(i):
        pair = (i + 1) // 2
        return side(i + jnp.where(pair == 1, 2, jnp.where(pair == 2, -2, 0)))

    def spread(j):
        def body(i):
            @pl.when(i > 0)
            def _():
                z_here(j, turn(i)).wait_recv()

            @pl.when(i == 1)
            def _():
                z_pass(j, 2, 1).start()

                @pl.when(back_z(2) % 2 == 0)
                def _():
                    z_pass(j, 2, 2).start()

            @pl.when(i == 2)
            def _():
                z_pass(j, 6, 7).start()

                @pl.when(back_z(6) % 2 == 1)
                def _():
                    z_pass(j, 6, 6).start()

            piece = back_z(turn(i))
            for a in range(2):

                @pl.when(piece % 2 == a)
                def _():
                    for axis in (a, 1 - a):
                        for d in (1, 3, 2) if axis == a else (2, 1, 3):
                            n_copy(j, axis, d, piece // 2, a).start()

        loop(0, 8, body)

    def forward(j):
        def body(i):
            piece = back_z(turn(i))
            n, a = piece // 2, piece % 2
            group(gx.at[j, :, y, n, a], n_r.at[j, n, a]).wait_recv()
            b = 1 - a
            for e, goals in ((1, (1, 3)), (3, (1, 3)), (2, (1, 3, 2))):
                for d in goals:
                    f_copy(j, n, a, b * e, a * e, a * d, b * d).start()
            for d in (1, 3):
                f_copy(j, n, a, 2 * a, 2 * b, b * d, a * d).start()

        loop(0, 8, body)
        group(gx.at[j, 0:2, 0], o_r.at[j]).wait_recv()

    def take(j, e):
        loop(0, 4, lambda d: split(j, e, d))

    def cross(j):
        for e in (0, 1, 3):
            if e:
                group(gx.at[j, x, 0:3], f_r.at[j, (e - 1) // 2]).wait_recv()
            x_copy(j, e).start()
            take(j, e)
        for d in (0, 1, 3, 2):
            if d:
                group(gx.at[j, x, y], f_r.at[j, 1 + d]).wait_recv()
            x_copy(j, 2, d).start()
            split(j, 2, d)

    @pl.when(pump)
    def _():
        loop(1, 8, lambda d: c_copy(d).start())
        p_near(0)
        both_ways(lambda s: p_far(s, 4, 0))
        both_ways(lambda s: p_far(s, 3, 0))
        partial()
        u_send(0)
        loads[3].wait()
        swap().start()
        group(p_v.at[0:3], h_r.at[0]).wait_recv()
        both_ways(lambda s: p_far(s, 4, 1))
        both_ways(lambda s: p_far(s, 3, 1))
        both_ways(lambda s: p_far(s, 2, 0))
        group(p_v.at[0:4], h_r.at[1]).wait_recv()
        both_ways(lambda s: p_far(s, 2, 1))
        p_near(1)

        d_copy.wait_recv()
        group(cz.at[0:15], c_r).wait_recv()
        both = jnp.concatenate([d_v[1], d_t[...]], axis=0)
        for n in range(8):
            upper = jnp.concatenate([cz[2 * n][:, :64], cz[2 * n + 1][:, :64]], axis=1)
            lower = jnp.concatenate([cz[2 * n][:, 64:], cz[2 * n + 1][:, 64:]], axis=1)
            e = precise(both, jnp.concatenate([upper, lower], axis=0))
            es[2 * n] = e[:64]
            es[2 * n + 1] = e[64:]
        loop(1, 16, lambda d: e_copy(d).start())
        u_send(1)

        both_ways(lambda s: p_pass(s, 4, 1))

        group(er.at[1:16], e_r).wait_recv()
        er[0] = es[r]
        eg[r // 2] = sum(er[d] for d in range(16))
        loop(0, 8, lambda d: g_copy(d).start())
        both_ways(lambda s: p_pass(s, 3, 1))
        both_ways(lambda s: p_pass(s, 2, 1))
        both_ways(lambda s: p_pass(s, 4, 2))
        both_ways(lambda s: p_pass(s, 3, 2))
        both_ways(lambda s: p_pass(s, 4, 3))

        for j in range(2):
            for e in (0, 1, 3):
                x_copy(j, e).wait_recv()
                take(j, e)
            for d in (0, 1, 3, 2):
                x_copy(j, 2, d).wait_recv()
                split(j, 2, d)

    @pl.when(chain)
    def _():
        u_send(0)
        loop(0, 8, lambda d: c_copy(d).start())
        d_copy.start()
        loads[3].wait()
        swap().start()
        loop(0, 14, lambda i: hand(i // 2, i % 2).start())

        group(ur.at[0], u_r.at[0]).wait_recv()
        gx[0, x, y, z // 2, z % 2] = sum(ur[0, i] for i in range(16))
        z_send(0)
        u_send(1)
        spread(0)
        forward(0)

        group(ur.at[1], u_r.at[1]).wait_recv()
        total = sum(ur[1, i] for i in range(16))
        tile = [gx[0, x, 2 * (y // 2) + hh, n // 2, n % 2] for n in range(8) for hh in range(2)]
        group(eg, g_r).wait_recv()
        e = jnp.concatenate([eg[n] for n in range(8)], axis=1)
        gx[1, x, y, z // 2, z % 2] = total - precise(e, jnp.concatenate(tile, axis=0))
        z_send(1)
        spread(1)
        cross(0)
        forward(1)
        cross(1)

    for n in range(8):
        for j in range(2):
            adj_v[j, :, 128 * n : 128 * n + 128] = gx[j, n // 2, 2 * (n % 2) + k, z // 2, z % 2]
    adj_out = pltpu.make_async_copy(adj_v, adj_ref, st.at[0])
    adj_out.start()

    swap().wait_send()

    @pl.when(pump)
    def _():
        group(cz.at[0:7], c_s).wait_send()
        group(us, u_s).wait_send()
        group(es.at[0:15], e_s).wait_send()
        group(eg, g_s).wait_send()

    @pl.when(chain)
    def _():
        group(cz.at[0:8], c_s).wait_send()

        @pl.when(h == 0)
        def _():
            group(us, u_s).wait_send()

        @pl.when(h == 1)
        def _():
            group(us.at[:, 0:7], u_s).wait_send()

        d_copy.wait_send()
        group(p_v.at[0:7], h_s).wait_send()
        group(er.at[0:14], z_s).wait_send()
        group(gx.at[0, 0:3], n_s).wait_send()
        for j in range(2):
            group(gx.at[j, 0:3, 0:3], f_s.at[j]).wait_send()

    loads[4].wait()
    loads[5].wait()
    swap().wait_recv()
    out = [
        pltpu.make_async_copy(o_v.at[:, 256 * n : 256 * n + 256], out_ref.at[:, 256 * n : 256 * n + 256], st.at[1])
        for n in range(4)
    ]

    def update(there, last):
        block = jnp.concatenate([pr_v[there, 0], pr_v[there, 1]], axis=1)
        high = block.astype(BF16)
        low = (block - high.astype(F32)).astype(BF16)
        both = jnp.concatenate([high, low], axis=0)
        for n in range(4):
            x_high = jnp.concatenate([xh[2 * n + i, there].reshape(256, 128) for i in range(2)], axis=1)
            x_low = jnp.concatenate([xl[2 * n + i, there].reshape(256, 128) for i in range(2)], axis=1)
            one, two = coarse(both, x_high), coarse(high, x_low)
            o_v[:, 256 * n : 256 * n + 256] -= one[:256] + (two + one[256:])
            if last:
                out[n].start()

    update(z, False)

    def step(i):
        p_here(i).wait_recv()
        update(back_z(side(i)), False)

    loop(1, 7, step)
    group(pr_v.at[back_z(4)], p_r.at[k, 4]).wait_recv()
    update(back_z(4), True)

    @pl.when(pump)
    def _():
        for s in range(2):
            group(gx.at[0], p_s.at[s]).wait_send()

    @pl.when(chain)
    def _():
        for j in range(2):
            group(gx.at[j], x_s.at[j]).wait_send()

    adj_out.wait()
    group(o_v, st.at[1]).wait_recv()


def settle(adj_ref, out_ref, adj_to, out_to, adj_v, out_v, in_s, to_s):
    parts = [(out_ref, out_v, out_to, pl.ds(64 * i, 64), 0) for i in range(4)]
    parts += [(adj_ref, adj_v, adj_to, pl.ds(i, 1), 1) for i in range(2)]
    loads = [pltpu.make_async_copy(src.at[at], held.at[at], in_s.at[i]) for i, (src, held, _, at, _) in enumerate(parts)]
    for load in loads:
        load.start()
    for load, (_, held, to, at, n) in zip(loads, parts):
        load.wait()
        pltpu.make_async_copy(held.at[at], to.at[at], to_s.at[n]).start()
    pltpu.make_async_copy(out_v, out_to, to_s.at[0]).wait()
    pltpu.make_async_copy(adj_v, adj_to, to_s.at[1]).wait()


def body(diag_inverse, coupling, rhs_top, panel, rhs_rest):
    vmem, sem = pltpu.VMEM, pltpu.SemaphoreType.DMA
    scratch = [
        vmem((2, 64, 64), F32), vmem((64, 64), F32), vmem((2, 64, 1024), F32), vmem((16, 2, 256, 128), F32),
        vmem((8, 2, 256, 128), F32), vmem((256, 1024), F32), vmem((2, 64, 1024), F32), vmem((64, 64), F32),
        vmem((16, 32, 128), F32), vmem((2, 8, 64, 128), F32), vmem((2, 16, 64, 128), F32),
        vmem((16, 64, 128), F32), vmem((16, 64, 128), F32), vmem((8, 64, 128), F32),
        vmem((2, 4, 4, 4, 2, 64, 128), F32), vmem((8, 8, 2, 2, 64, 128), BF16), vmem((8, 8, 2, 2, 64, 128), BF16),
        vmem((2, 3, 2, 2, 256, 128), F32), vmem((2, 3, 2, 256, 128), F32),
        sem((6,)), sem((2,)), sem((2,)), sem((2, 5)), sem((2, 6)), sem, sem((2,)), sem, sem, sem, sem, sem, sem,
        sem, sem((2,)), sem, sem, sem, sem, sem, sem((2, 8)),
        sem, sem((2, 4, 2)), sem((2,)), sem((2,)), sem((2, 5)), sem((2,)), sem((2, 7)),
    ]
    shapes = (jax.ShapeDtypeStruct((2, 64, 1024), F32), jax.ShapeDtypeStruct((256, 1024), F32))
    results = pl.pallas_call(
        kernel,
        out_shape=shapes,
        in_specs=[pl.BlockSpec(memory_space=pl.ANY)] * 5,
        out_specs=[pl.BlockSpec(memory_space=pl.ANY)] * 2,
        scratch_shapes=scratch,
        compiler_params=pltpu.CompilerParams(collective_id=0, has_side_effects=True, vmem_limit_bytes=60 * 2**20),
        name="window",
    )(diag_inverse, coupling, rhs_top, panel.reshape(16, 256, 128), rhs_rest)
    return pl.pallas_call(
        settle,
        out_shape=shapes,
        in_specs=[pl.BlockSpec(memory_space=pl.ANY)] * 2,
        out_specs=[pl.BlockSpec(memory_space=pl.ANY)] * 2,
        scratch_shapes=[vmem((2, 64, 1024), F32), vmem((256, 1024), F32), sem((6,)), sem((2,))],
        compiler_params=pltpu.CompilerParams(vmem_limit_bytes=60 * 2**20),
        name="settle",
    )(*results)


def solution(mesh):
    in_specs = (
        P(None, "pcol", "prow"),
        P("prow", "pcol"),
        P(None, "prow", None),
        P("prow", "pcol"),
        P(("prow", "pcol"), None),
    )
    out_specs = (P(None, "pcol", None), P(("prow", "pcol"), None))
    return jax.shard_map(body, mesh=mesh, in_specs=in_specs, out_specs=out_specs, check_vma=False)
```

```python
import jax
import jax.numpy as jnp
from jax import lax
from jax.experimental import pallas as pl
from jax.experimental.pallas import tpu as pltpu
from jax.sharding import PartitionSpec as P

MESH = pl.DeviceIdType.MESH
F32, BF16 = jnp.float32, jnp.bfloat16


def precise(a, b):
    return jnp.dot(a, b, precision=lax.Precision.HIGHEST, preferred_element_type=F32)


def coarse(a, b):
    return jnp.dot(a, b, preferred_element_type=F32)


def remote(src, dst, send, recv, device):
    return pltpu.make_async_remote_copy(
        src_ref=src, dst_ref=dst, send_sem=send, recv_sem=recv, device_id=device, device_id_type=MESH
    )


def loop(low, high, body):
    def step(i, carry):
        body(i)
        return carry

    lax.fori_loop(low, high, step, 0)


def kernel(
    d_ref, c_ref, b_ref, p_ref, rest_ref, adj_ref, out_ref,
    d_v, c_v, b_v, p_v, pr_v, o_v, adj_v, d_t,
    cz, us, ur, es, er, eg, gx, xh, xl, tf, th,
    ld, st, p_s, p_r, t_r, h_s, h_r, w_s, w_r, d_s, d_r, c_s, c_r, u_s, u_r, e_s, e_r, g_s, g_r, z_s, z_r, n_s, n_r, o_r, f_s, f_r, x_s, x_r,
):
    r, c = lax.axis_index("prow"), lax.axis_index("pcol")
    x, y, z, k = r // 4, r % 4, c // 2, c % 2
    h = r % 2
    twin = c + 1 - 2 * k
    pump, chain = k == 0, k == 1

    def row(d):
        return (r + d) % 16

    def at_z(d):
        return (z + d) % 8

    def back_z(d):
        return (z + 8 - d) % 8

    loads = [
        pltpu.make_async_copy(src, dst, ld.at[i])
        for i, (src, dst) in enumerate(
            [(d_ref, d_v), (c_ref, c_v), (b_ref, b_v), (p_ref, p_v.at[:, 0]), (rest_ref, o_v), (p_ref.at[c], pr_v.at[z, k])]
        )
    ]
    for load in loads:
        load.start()

    barrier = pltpu.get_barrier_semaphore()

    def greet(*device):
        pl.semaphore_signal(barrier, inc=1, device_id=device, device_id_type=MESH)

    greet(r, twin)
    loop(2, 16, lambda d: greet(r, (2 * z + d) % 16))

    loop(1, 16, lambda d: greet(row(d), c))

    @pl.when(chain & (h == 0))
    def _():
        loop(1, 16, lambda d: greet(row(d), twin))

    @pl.when(chain & (h == 1))
    def _():
        loop(1, 8, lambda d: greet(row(2 * d), twin))

    def partial():
        loads[2].wait()
        for j in range(2):
            u = precise(d_v[j], b_v[j])
            for n in range(8):
                us[j, n] = u[:, 128 * n : 128 * n + 128]

    for load in loads[:2]:
        load.wait()
    cz[c] = jnp.concatenate([c_v[:32], c_v[32:]], axis=1)

    @pl.when(chain)
    def _():
        partial()

    @pl.when(chain & (h == 1))
    def _():
        for j in range(2):
            pltpu.make_async_copy(us.at[j, r // 2], ur.at[j, r], u_r.at[j]).start()

    @pl.when(pump)
    def _():
        pl.semaphore_wait(barrier, 37 + 8 * h)

    @pl.when(chain)
    def _():
        pl.semaphore_wait(barrier, 30)

    def ahead(s, d):
        return (z + d * (1 + 6 * s)) % 8

    def behind(s, d):
        return (z + d * (7 - 6 * s)) % 8

    def p_near(kk):
        for s in range(2):
            for i in range(2):
                q = 2 * ahead(s, 1) + i
                block = p_v.at[q, 1] if kk else p_ref.at[q]
                remote(block, pr_v.at[z, kk], p_s.at[s], p_r.at[s, 1], (r, q)).start()

    def p_far(s, d, kk):
        goal = 2 * ahead(s, 4) + s if d == 4 else pl.ds(2 * ahead(s, d), 2)
        block = p_v.at[goal, 1] if kk else p_ref.at[goal]
        held = th.at[s, 0, kk] if d == 4 else tf.at[s, 3 - d, :, kk]
        remote(block, held, p_s.at[s], t_r.at[s, 4 - d], (r, 2 * ahead(s, 1))).start()

    def p_pass(s, d, n):
        to = 2 * ahead(s, 1)
        if d == 4:
            held, sem = th.at[s, n - 1], t_r.at[s, (0, 3, 5)[n - 1]]
        else:
            held, sem = (tf.at[s, 3 - d], t_r.at[s, 4 - d]) if n == 1 else (tf.at[s, 2], t_r.at[s, 4])
        group(held, sem).wait_recv()
        if n < d - 1:
            on, sem = (th.at[s, n], t_r.at[s, (3, 5)[n - 1]]) if d == 4 else (tf.at[s, 2], t_r.at[s, 4])
            remote(held, on, p_s.at[s], sem, (r, to)).start()
        elif d == 4:
            remote(held, pr_v.at[behind(s, n)], p_s.at[s], p_r.at[s, 4], (r, to + s)).start()
        else:
            for i in range(2):
                remote(held.at[i], pr_v.at[behind(s, n)], p_s.at[s], p_r.at[s, d], (r, to + i)).start()

    def both_ways(body):
        for s in range(2):
            body(s)

    def p_here(i):
        d, s = (i + 1) // 2, (i + 1) % 2
        block = pr_v.at[back_z(side(i))]
        return group(block, p_r.at[s, d])

    def hand(n, i):
        q = 2 * at_z((4 + (2 * (n % 2) - 1) * ((n + 1) // 2)) % 8) + i
        return remote(p_v.at[q, 0], p_v.at[q, 1], h_s, h_r.at[(n + 1) // 4], (r, twin))

    def swap():
        return remote(p_v.at[twin, 0], pr_v.at[z, k], w_s, w_r, (r, twin))

    def group(block, sem):
        return remote(block, block, sem, sem, (r, twin))

    d_copy = remote(d_v.at[1], d_t, d_s, d_r, (r, twin))

    def c_copy(d):
        return remote(cz.at[c], cz.at[c], c_s, c_r, (r, 2 * at_z(d)))

    def u_send(j):
        def body(n):
            @pl.when(pump | (2 * n + 1 != r))
            def _():
                remote(us.at[j, n], ur.at[j, r], u_s, u_r.at[j], (2 * n + k, 2 * z + 1)).start()

        loop(0, 8, body)

    def e_copy(d):
        return remote(es.at[row(d)], er.at[d], e_s, e_r, (row(d), c))

    def g_copy(d):
        return remote(eg.at[r // 2], eg.at[r // 2], g_s, g_r, (row(2 * d), 2 * z + 1))

    def z_copy(j, d):
        block = gx.at[j, x, y, z // 2, z % 2]
        return remote(block, block, z_s, z_r.at[j, d], (r, 2 * at_z(d) + k))

    def z_pass(j, d, on):
        block = gx.at[j, x, y, back_z(d) // 2, back_z(d) % 2]
        return remote(block, block, z_s, z_r.at[j, (d + on) % 8], (r, 2 * at_z(on) + k))

    def z_here(j, d):
        block = gx.at[j, x, y, back_z(d) // 2, back_z(d) % 2]
        return remote(block, block, z_s, z_r.at[j, d], (r, c))

    def along(axis, d):
        return (((x + d) % 4) * 4 + y, c) if axis == 0 else (x * 4 + (y + d) % 4, c)

    def n_copy(j, axis, d, i, a):
        block = gx.at[j, x, y, i, a]
        sem = n_r.at[j, i, a] if axis == a or d == 2 else o_r.at[j]
        return remote(block, block, n_s, sem, along(axis, d))

    def f_copy(j, i, a, dx, dy, mx, my):
        block = gx.at[j, (x + 4 - dx) % 4, (y + 4 - dy) % 4, i, a]
        across, down = (dx + mx) % 4, (dy + my) % 4
        sem = f_r.at[j, jnp.where(across == 2, 1 + down, (across - 1) // 2)]
        return remote(block, block, f_s.at[j], sem, (((x + mx) % 4) * 4 + (y + my) % 4, c))

    def x_copy(j, e, d=None):
        block = gx.at[j, (x + 4 - e) % 4] if d is None else gx.at[j, (x + 4 - e) % 4, (y + 4 - d) % 4]
        return remote(block, block, x_s.at[j], x_r.at[j, (e + 1) // 2 if d is None else 3 + d], (r, twin))

    def split(j, e, d):
        xx, yy = (x + 4 - e) % 4, (y + 4 - d) % 4
        p, hh = 2 * xx + yy // 2, yy % 2

        def body(i):
            value = gx[j, xx, yy, i // 2, i % 2]
            high = value.astype(BF16)
            xh[p, i, hh, j] = high
            xl[p, i, hh, j] = (value - high.astype(F32)).astype(BF16)

        loop(0, 8, body)

    def side(i):
        return ((2 * (i % 2) - 1) * ((i + 1) // 2) + 8) % 8

    def z_send(j):
        for d in (2, 6, 1, 7):
            z_copy(j, d).start()

    def turn(i):
        pair = (i + 1) // 2
        return side(i + jnp.where(pair == 1, 2, jnp.where(pair == 2, -2, 0)))

    def spread(j):
        def body(i):
            @pl.when(i > 0)
            def _():
                z_here(j, turn(i)).wait_recv()

            @pl.when(i == 1)
            def _():
                z_pass(j, 2, 1).start()

                @pl.when(back_z(2) % 2 == 0)
                def _():
                    z_pass(j, 2, 2).start()

            @pl.when(i == 2)
            def _():
                z_pass(j, 6, 7).start()

                @pl.when(back_z(6) % 2 == 1)
                def _():
                    z_pass(j, 6, 6).start()

            piece = back_z(turn(i))
            for a in range(2):

                @pl.when(piece % 2 == a)
                def _():
                    for axis in (a, 1 - a):
                        for d in (1, 3, 2) if axis == a else (2, 1, 3):
                            n_copy(j, axis, d, piece // 2, a).start()

        loop(0, 8, body)

    def forward(j):
        def body(i):
            piece = back_z(turn(i))
            n, a = piece // 2, piece % 2
            group(gx.at[j, :, y, n, a], n_r.at[j, n, a]).wait_recv()
            b = 1 - a
            for e, goals in ((1, (1, 3)), (3, (1, 3)), (2, (1, 3, 2))):
                for d in goals:
                    f_copy(j, n, a, b * e, a * e, a * d, b * d).start()
            for d in (1, 3):
                f_copy(j, n, a, 2 * a, 2 * b, b * d, a * d).start()

        loop(0, 8, body)
        group(gx.at[j, 0:2, 0], o_r.at[j]).wait_recv()

    def take(j, e):
        loop(0, 4, lambda d: split(j, e, d))

    def cross(j):
        for e in (0, 1, 3):
            if e:
                group(gx.at[j, x, 0:3], f_r.at[j, (e - 1) // 2]).wait_recv()
            x_copy(j, e).start()
            take(j, e)
        for d in (0, 1, 3, 2):
            if d:
                group(gx.at[j, x, y], f_r.at[j, 1 + d]).wait_recv()
            x_copy(j, 2, d).start()
            split(j, 2, d)

    @pl.when(pump)
    def _():
        loop(1, 8, lambda d: c_copy(d).start())
        p_near(0)
        both_ways(lambda s: p_far(s, 4, 0))
        both_ways(lambda s: p_far(s, 3, 0))
        partial()
        u_send(0)
        loads[3].wait()
        swap().start()
        group(p_v.at[0:3], h_r.at[0]).wait_recv()
        both_ways(lambda s: p_far(s, 4, 1))
        both_ways(lambda s: p_far(s, 3, 1))
        both_ways(lambda s: p_far(s, 2, 0))
        group(p_v.at[0:4], h_r.at[1]).wait_recv()
        both_ways(lambda s: p_far(s, 2, 1))
        p_near(1)

        d_copy.wait_recv()
        group(cz.at[0:15], c_r).wait_recv()
        both = jnp.concatenate([d_v[1], d_t[...]], axis=0)
        for n in range(8):
            upper = jnp.concatenate([cz[2 * n][:, :64], cz[2 * n + 1][:, :64]], axis=1)
            lower = jnp.concatenate([cz[2 * n][:, 64:], cz[2 * n + 1][:, 64:]], axis=1)
            e = precise(both, jnp.concatenate([upper, lower], axis=0))
            es[2 * n] = e[:64]
            es[2 * n + 1] = e[64:]
        loop(1, 16, lambda d: e_copy(d).start())
        u_send(1)

        both_ways(lambda s: p_pass(s, 4, 1))

        group(er.at[1:16], e_r).wait_recv()
        er[0] = es[r]
        eg[r // 2] = sum(er[d] for d in range(16))
        loop(0, 8, lambda d: g_copy(d).start())
        both_ways(lambda s: p_pass(s, 3, 1))
        both_ways(lambda s: p_pass(s, 2, 1))
        both_ways(lambda s: p_pass(s, 4, 2))
        both_ways(lambda s: p_pass(s, 3, 2))
        both_ways(lambda s: p_pass(s, 4, 3))

        for j in range(2):
            for e in (0, 1, 3):
                x_copy(j, e).wait_recv()
                take(j, e)
            for d in (0, 1, 3, 2):
                x_copy(j, 2, d).wait_recv()
                split(j, 2, d)

    @pl.when(chain)
    def _():
        u_send(0)
        loop(0, 8, lambda d: c_copy(d).start())
        d_copy.start()
        loads[3].wait()
        swap().start()
        loop(0, 14, lambda i: hand(i // 2, i % 2).start())

        group(ur.at[0], u_r.at[0]).wait_recv()
        gx[0, x, y, z // 2, z % 2] = sum(ur[0, i] for i in range(16))
        z_send(0)
        u_send(1)
        spread(0)
        forward(0)

        group(ur.at[1], u_r.at[1]).wait_recv()
        total = sum(ur[1, i] for i in range(16))
        tile = [gx[0, x, 2 * (y // 2) + hh, n // 2, n % 2] for n in range(8) for hh in range(2)]
        group(eg, g_r).wait_recv()
        e = jnp.concatenate([eg[n] for n in range(8)], axis=1)
        gx[1, x, y, z // 2, z % 2] = total - precise(e, jnp.concatenate(tile, axis=0))
        z_send(1)
        spread(1)
        cross(0)
        forward(1)
        cross(1)

    for n in range(8):
        for j in range(2):
            adj_v[j, :, 128 * n : 128 * n + 128] = gx[j, n // 2, 2 * (n % 2) + k, z // 2, z % 2]
    adj_out = pltpu.make_async_copy(adj_v, adj_ref, st.at[0])
    adj_out.start()

    swap().wait_send()

    @pl.when(pump)
    def _():
        group(cz.at[0:7], c_s).wait_send()
        group(us, u_s).wait_send()
        group(es.at[0:15], e_s).wait_send()
        group(eg, g_s).wait_send()

    @pl.when(chain)
    def _():
        group(cz.at[0:8], c_s).wait_send()

        @pl.when(h == 0)
        def _():
            group(us, u_s).wait_send()

        @pl.when(h == 1)
        def _():
            group(us.at[:, 0:7], u_s).wait_send()

        d_copy.wait_send()
        group(p_v.at[0:7], h_s).wait_send()
        group(er.at[0:14], z_s).wait_send()
        group(gx.at[0, 0:3], n_s).wait_send()
        for j in range(2):
            group(gx.at[j, 0:3, 0:3], f_s.at[j]).wait_send()

    loads[4].wait()
    loads[5].wait()
    swap().wait_recv()
    out = [
        pltpu.make_async_copy(o_v.at[:, 256 * n : 256 * n + 256], out_ref.at[:, 256 * n : 256 * n + 256], st.at[1])
        for n in range(4)
    ]

    def update(there, last):
        block = jnp.concatenate([pr_v[there, 0], pr_v[there, 1]], axis=1)
        high = block.astype(BF16)
        low = (block - high.astype(F32)).astype(BF16)
        both = jnp.concatenate([high, low], axis=0)
        for n in range(4):
            x_high = jnp.concatenate([xh[2 * n + i, there].reshape(256, 128) for i in range(2)], axis=1)
            x_low = jnp.concatenate([xl[2 * n + i, there].reshape(256, 128) for i in range(2)], axis=1)
            one, two = coarse(both, x_high), coarse(high, x_low)
            o_v[:, 256 * n : 256 * n + 256] -= one[:256] + (two + one[256:])
            if last:
                out[n].start()

    update(z, False)

    def step(i):
        p_here(i).wait_recv()
        update(back_z(side(i)), False)

    loop(1, 7, step)
    group(pr_v.at[back_z(4)], p_r.at[k, 4]).wait_recv()
    update(back_z(4), True)

    @pl.when(pump)
    def _():
        for s in range(2):
            group(gx.at[0], p_s.at[s]).wait_send()

    @pl.when(chain)
    def _():
        for j in range(2):
            group(gx.at[j], x_s.at[j]).wait_send()

    adj_out.wait()
    group(o_v, st.at[1]).wait_recv()


def settle(adj_ref, out_ref, adj_to, out_to, adj_v, out_v, in_s, to_s):
    parts = [(out_ref, out_v, out_to, pl.ds(128 * i, 128), 0) for i in range(2)]
    parts += [(adj_ref, adj_v, adj_to, pl.ds(0, 2), 1) for i in range(1)]
    loads = [pltpu.make_async_copy(src.at[at], held.at[at], in_s.at[i]) for i, (src, held, _, at, _) in enumerate(parts)]
    for load in loads:
        load.start()
    for load, (_, held, to, at, n) in zip(loads, parts):
        load.wait()
        pltpu.make_async_copy(held.at[at], to.at[at], to_s.at[n]).start()
    pltpu.make_async_copy(out_v, out_to, to_s.at[0]).wait()
    pltpu.make_async_copy(adj_v, adj_to, to_s.at[1]).wait()


def body(diag_inverse, coupling, rhs_top, panel, rhs_rest):
    vmem, sem = pltpu.VMEM, pltpu.SemaphoreType.DMA
    scratch = [
        vmem((2, 64, 64), F32), vmem((64, 64), F32), vmem((2, 64, 1024), F32), vmem((16, 2, 256, 128), F32),
        vmem((8, 2, 256, 128), F32), vmem((256, 1024), F32), vmem((2, 64, 1024), F32), vmem((64, 64), F32),
        vmem((16, 32, 128), F32), vmem((2, 8, 64, 128), F32), vmem((2, 16, 64, 128), F32),
        vmem((16, 64, 128), F32), vmem((16, 64, 128), F32), vmem((8, 64, 128), F32),
        vmem((2, 4, 4, 4, 2, 64, 128), F32), vmem((8, 8, 2, 2, 64, 128), BF16), vmem((8, 8, 2, 2, 64, 128), BF16),
        vmem((2, 3, 2, 2, 256, 128), F32), vmem((2, 3, 2, 256, 128), F32),
        sem((6,)), sem((2,)), sem((2,)), sem((2, 5)), sem((2, 6)), sem, sem((2,)), sem, sem, sem, sem, sem, sem,
        sem, sem((2,)), sem, sem, sem, sem, sem, sem((2, 8)),
        sem, sem((2, 4, 2)), sem((2,)), sem((2,)), sem((2, 5)), sem((2,)), sem((2, 7)),
    ]
    shapes = (jax.ShapeDtypeStruct((2, 64, 1024), F32), jax.ShapeDtypeStruct((256, 1024), F32))
    results = pl.pallas_call(
        kernel,
        out_shape=shapes,
        in_specs=[pl.BlockSpec(memory_space=pl.ANY)] * 5,
        out_specs=[pl.BlockSpec(memory_space=pl.ANY)] * 2,
        scratch_shapes=scratch,
        compiler_params=pltpu.CompilerParams(collective_id=0, has_side_effects=True, vmem_limit_bytes=60 * 2**20),
        name="window",
    )(diag_inverse, coupling, rhs_top, panel.reshape(16, 256, 128), rhs_rest)
    return pl.pallas_call(
        settle,
        out_shape=shapes,
        in_specs=[pl.BlockSpec(memory_space=pl.ANY)] * 2,
        out_specs=[pl.BlockSpec(memory_space=pl.ANY)] * 2,
        scratch_shapes=[vmem((2, 64, 1024), F32), vmem((256, 1024), F32), sem((3,)), sem((2,))],
        compiler_params=pltpu.CompilerParams(vmem_limit_bytes=60 * 2**20),
        name="settle",
    )(*results)


def solution(mesh):
    in_specs = (
        P(None, "pcol", "prow"),
        P("prow", "pcol"),
        P(None, "prow", None),
        P("prow", "pcol"),
        P(("prow", "pcol"), None),
    )
    out_specs = (P(None, "pcol", None), P(("prow", "pcol"), None))
    return jax.shard_map(body, mesh=mesh, in_specs=in_specs, out_specs=out_specs, check_vma=False)
```
